128 devices in a mesh: context: 8 (over z, core), dp: 4 (over y), head: 4 (over x).
Axes of the slice: x: 4, y: 4, z: 4, core: 2. Of those that a mesh axis runs over, the one named last changes fastest.
Arguments:
- inputs: bfloat16 [4, 1024, 2304], P('dp', 'context', 'head'), may hold values from -6 to 6
- output_grad: bfloat16 [4, 1024, 2304], P('dp', 'context', 'head'), may hold values from -6 to 6
- qkv_weight: bfloat16 [2304, 3, 4096], P(None, None, 'head'), may hold values from -0.125 to 0.125
- out_weight: bfloat16 [2304, 4096], P(None, 'head'), may hold values from -0.09375 to 0.09375
- down_weight: bfloat16 [2304, 128], replicated, may hold values from -0.125 to 0.125
- up_weight: bfloat16 [128, 4096], P(None, 'head'), may hold values from -0.5 to 0.5
- beta_weight: bfloat16 [2304, 32], P(None, 'head'), may hold values from -0.125 to 0.125
- gate_bias: float32 [4096], P('head'), may hold values from -9 to -1.6, as said below
Outputs:
- layer_out: bfloat16 [4, 1024, 2304], P('dp', 'context', 'head')
- input_grad: bfloat16 [4, 1024, 2304], P('dp', 'context', 'head')
- qkv_grad: bfloat16 [2304, 3, 4096], P(('context', 'dp'), None, 'head')
- out_grad: bfloat16 [2304, 4096], P(('context', 'dp'), 'head')
- up_grad: float32 [128, 4096], P(None, 'head')
- down_grad: float32 [2304, 128], replicated
- beta_grad: float32 [2304, 32], P(None, 'head')
- bias_grad: float32 [4096], P('head')
The draws below stay inside these ranges and needn't reach their ends.
Inputs may be any that keep to these rules, and one draw needn't show every extreme that they name: `gate_bias`: offsets of the decay gate, one per channel.
All inputs are finite; a program needn't handle non-finite values.
Results may differ from the reference program's by a relative error of at most 0.02.
Values may be sent and summed in bfloat16 or wider, within the bound.
No kernel may reach another device: no remote copies, remote signals or barrier semaphores. Data moves between devices by JAX's collectives and lax.ppermute only.
A program may use at most 192 MiB of HBM per device.

```python
import math
import jax
import jax.numpy as jnp
from jax import lax

D = 2304
H = 32
DK = 128
RANK = 128
SPAN = 64
TOK_DEV = 128
SEQS = 4
LENGTH = 1024
N_HEAD = 4


def draw_gate_bias(key, part):
    choose_key, slow_key, fast_key = jax.random.split(key, 3)
    channels = H * DK
    fast_share = 0.5
    picked = jax.random.uniform(choose_key, (channels,), jnp.float32) < fast_share
    slow_rate = jnp.exp(jax.random.uniform(slow_key, (channels,), jnp.float32, math.log(0.3 / LENGTH), math.log(1.0 / LENGTH)))
    fast_rate = jnp.exp(jax.random.uniform(fast_key, (channels,), jnp.float32, math.log(1.0 / 60.0), math.log(1.0 / 25.0)))
    fraction = 4.0 * jnp.where(picked, fast_rate, slow_rate)
    return jnp.log(fraction / (1.0 - fraction)).astype(jnp.float32)


def block_scale(rng, extent, cuts, smallest, largest):
    factor_of = 1.0
    for position, parts in cuts:
        draws = jax.random.uniform(jax.random.fold_in(jax.random.fold_in(rng, 6), position), (parts,), jnp.float32, smallest / len(cuts), largest / len(cuts))
        factor_of = factor_of * jnp.repeat(jnp.exp(draws), extent[position] // parts).reshape((-1,) + (1,) * (len(extent) - 1 - position))
    return factor_of


def normal_values(stream_key, shape, width, reach, shards=(), kind=jnp.bfloat16):
    drawn = width * jax.random.normal(stream_key, shape, jnp.float32)
    if shards:
        drawn = drawn * block_scale(stream_key, shape, shards, -0.22, 0.18)
    return jnp.clip(drawn, -reach, reach).astype(kind)


def setup_inputs(seed: int = 0) -> dict:
    splits = jax.random.split(jax.random.key(seed), 9)
    inputs = normal_values(splits[0], (SEQS, LENGTH, D), 1.0, 6.0, ((0, 4), (1, 8), (2, 4)))
    output_grad = normal_values(splits[1], (SEQS, LENGTH, D), 1.0, 6.0, ((0, 4), (1, 8), (2, 4)))
    qkv_weight = normal_values(splits[2], (D, 3, H * DK), D ** -0.5, 0.125, ((2, 4),))
    out_weight = normal_values(splits[3], (D, H * DK), (H * DK) ** -0.5, 0.09375, ((1, 4),))
    down_weight = normal_values(splits[4], (D, RANK), D ** -0.5, 0.125)
    up_weight = normal_values(splits[5], (RANK, H * DK), RANK ** -0.5, 0.5, ((1, 4),))
    beta_weight = normal_values(splits[6], (D, H), D ** -0.5, 0.125, ((1, 4),))
    gate_bias = draw_gate_bias(jax.random.fold_in(splits[8], 71), 0)
    return dict(inputs=inputs, output_grad=output_grad, qkv_weight=qkv_weight, out_weight=out_weight, down_weight=down_weight, up_weight=up_weight, beta_weight=beta_weight, gate_bias=gate_bias)


epsilon = 1e-06
highest = lax.Precision.HIGHEST

def product(pattern, left, right):
    return jnp.einsum(pattern, left, right, precision=highest)

def dense(left, right):
    return jnp.dot(left.astype(jnp.float32), right.astype(jnp.float32), preferred_element_type=jnp.float32)

def activate(projected, gate_pre, beta_logit):
    token_count = projected.shape[0]
    head_count = beta_logit.shape[1]
    head_width = projected.shape[2] // head_count
    blocks = projected.reshape(token_count, 3, head_count, head_width)

    def normalize(values):
        return values * lax.rsqrt(lax.optimization_barrier(jnp.sum(values * values, axis=-1, keepdims=True)) + epsilon)
    queries = jnp.swapaxes(normalize(blocks[:, 0]), 0, 1)
    key_rows = jnp.swapaxes(normalize(blocks[:, 1]), 0, 1)
    value_rows = jnp.swapaxes(blocks[:, 2], 0, 1)
    decays = jnp.swapaxes((-0.25 * jax.nn.sigmoid(gate_pre)).reshape(token_count, head_count, head_width), 0, 1)
    betas = jnp.swapaxes(jax.nn.sigmoid(beta_logit), 0, 1)
    return (queries, key_rows, value_rows, decays, betas)

def span_terms(queries, key_rows, value_rows, decays, betas):
    leading = queries.shape[:-2]
    block_count = queries.shape[-2] // SPAN

    def blocked(member):
        return member.reshape(leading + (block_count, SPAN) + member.shape[-1:])
    queries, key_rows, value_rows, decays = (blocked(queries), blocked(key_rows), blocked(value_rows), blocked(decays))
    betas = betas.reshape(leading + (block_count, SPAN))
    cumulative = jnp.cumsum(decays, axis=-2)
    middle = cumulative[..., SPAN // 2 - 1:SPAN // 2, :]
    final_decay = cumulative[..., SPAN - 1:, :]
    key_fwd = jnp.exp(cumulative - middle) * key_rows
    key_back = jnp.exp(middle - cumulative) * key_rows
    query_fwd = jnp.exp(cumulative - middle) * queries
    key_start = jnp.exp(cumulative) * key_rows
    query_start = jnp.exp(cumulative) * queries
    key_end = jnp.exp(final_decay - cumulative) * key_rows
    row_index = lax.broadcasted_iota(jnp.int32, (SPAN, SPAN), 0)
    col_index = lax.broadcasted_iota(jnp.int32, (SPAN, SPAN), 1)
    strict = (row_index > col_index).astype(jnp.float32)
    lower_mask = (row_index >= col_index).astype(jnp.float32)
    coupling = betas[..., :, None] * product('...tc,...sc->...ts', key_fwd, key_back) * strict
    powers = -coupling
    inverse = jnp.eye(SPAN, dtype=jnp.float32) + powers
    for section in range(1, (SPAN - 1).bit_length()):
        powers = product('...ts,...su->...tu', powers, powers)
        inverse = inverse + product('...ts,...su->...tu', inverse, powers)
    solver = inverse * betas[..., None, :]
    solved_values = product('...ts,...sc->...tc', solver, value_rows)
    solved_keys = product('...ts,...sc->...tc', solver, key_start)
    scores = product('...tc,...sc->...ts', query_fwd, key_back) * lower_mask
    query_eff = query_start - product('...ts,...sc->...tc', scores, solved_keys)
    local_out = product('...ts,...sc->...tc', scores, solved_values)
    side = queries.shape[-1]
    diagonal = jnp.eye(side, dtype=jnp.float32) * jnp.exp(final_decay)[..., 0, :, None]
    transition = diagonal - product('...sc,...sd->...cd', key_end, solved_keys)
    offset = product('...sc,...sd->...cd', key_end, solved_values)
    return (query_eff, local_out, transition, offset)

def chain(terms, state_in):

    def advance(carried, pieces):
        query_eff, local_out, transition, offset = pieces
        emitted = product('...tc,...cd->...td', query_eff, carried) + local_out
        return (product('...cd,...de->...ce', transition, carried) + offset, emitted)
    moved = tuple((jnp.moveaxis(member, -3, 0) for member in terms))
    final_state, emitted = lax.scan(advance, state_in, moved)
    return (jnp.moveaxis(emitted, 0, -3), final_state)

def reference(inputs, output_grad, qkv_weight, out_weight, down_weight, up_weight, beta_weight, gate_bias):
    seq_count, seq_len, model_width = inputs.shape
    flat_in = inputs.reshape(-1, model_width)
    token_count = flat_in.shape[0]
    all_width = qkv_weight.shape[2]
    head_count = beta_weight.shape[1]
    head_width = all_width // head_count
    qkv_flat = qkv_weight.reshape(model_width, 3 * all_width)
    projected = dense(flat_in, qkv_flat).reshape(token_count, 3, all_width)
    low_rank = dense(flat_in, down_weight).astype(jnp.bfloat16)
    gate_pre = dense(low_rank, up_weight) + gate_bias
    beta_logit = dense(flat_in, beta_weight)
    acts, act_vjp = jax.vjp(activate, projected, gate_pre, beta_logit)

    def per_sequence(queries, key_rows, value_rows, decays, betas):
        shaped = [member.reshape((head_count, seq_count, seq_len) + member.shape[2:]) for member in (queries, key_rows, value_rows, decays, betas)]
        return span_terms(*shaped)
    terms, terms_vjp = jax.vjp(per_sequence, *acts)
    start_state = jnp.zeros((head_count, seq_count, head_width, head_width), jnp.float32)
    (mixed_blocks, final_state), chain_vjp = jax.vjp(chain, terms, start_state)
    mixed = jnp.transpose(mixed_blocks.reshape(head_count, seq_count, seq_len, head_width), (1, 2, 0, 3))
    mixed = mixed.reshape(token_count, all_width).astype(jnp.bfloat16)
    layer_out = dense(mixed, out_weight.T).astype(jnp.bfloat16).reshape(inputs.shape)
    flat_grad = output_grad.reshape(-1, model_width)
    mixed_grad = dense(flat_grad, out_weight)
    grad_blocks = jnp.transpose(mixed_grad.reshape(seq_count, seq_len, head_count, head_width), (2, 0, 1, 3))
    grad_blocks = grad_blocks.reshape(mixed_blocks.shape)
    term_grads, unused_state = chain_vjp((grad_blocks, jnp.zeros_like(final_state)))
    proj_grad, pre_grad, logit_grad = act_vjp(terms_vjp(term_grads))
    proj_low = proj_grad.astype(jnp.bfloat16).reshape(token_count, 3 * all_width)
    gate_low = pre_grad.astype(jnp.bfloat16)
    logit_low = logit_grad.astype(jnp.bfloat16)
    group_width = all_width // N_HEAD
    input_part = dense(proj_low, qkv_flat.T) + dense(logit_low, beta_weight.T)
    down_grad = jnp.zeros((model_width, down_weight.shape[1]), jnp.float32)
    for group in range(N_HEAD):
        low_grad = dense(gate_low[:, group * group_width:(group + 1) * group_width], up_weight[:, group * group_width:(group + 1) * group_width].T).astype(jnp.bfloat16)
        input_part = input_part + dense(low_grad, down_weight.T)
        down_grad = down_grad + dense(flat_in.T, low_grad)
    input_grad = input_part.astype(jnp.bfloat16).reshape(inputs.shape)
    block_total = token_count // TOK_DEV

    def block_rows(member):
        return member.reshape(block_total, TOK_DEV, member.shape[-1])
    stacked = (block_rows(flat_in), block_rows(proj_low), block_rows(flat_grad), block_rows(mixed))

    def accumulate(carried, pieces):
        input_rows, proj_rows, grad_rows, mixed_rows = pieces
        first = lax.optimization_barrier(dense(input_rows.T, proj_rows).astype(jnp.bfloat16)).astype(jnp.float32)
        second = lax.optimization_barrier(dense(grad_rows.T, mixed_rows).astype(jnp.bfloat16)).astype(jnp.float32)
        return ((carried[0] + first, carried[1] + second), None)
    start_sums = (jnp.zeros((model_width, 3 * all_width), jnp.float32), jnp.zeros((model_width, all_width), jnp.float32))
    (qkv_sum, out_sum), unused_rows = lax.scan(accumulate, start_sums, stacked)
    qkv_grad = qkv_sum.reshape(model_width, 3, all_width).astype(jnp.bfloat16)
    out_grad = out_sum.astype(jnp.bfloat16)
    up_grad = dense(low_rank.T, gate_low)
    beta_grad = dense(flat_in.T, logit_low)
    bias_grad = lax.optimization_barrier(jnp.sum(pre_grad, axis=0))
    return (layer_out, input_grad, qkv_grad, out_grad, up_grad, down_grad, beta_grad, bias_grad)
```

```python
import functools
import jax
import jax.numpy as jnp
from jax import lax
from jax.experimental import pallas as pl
from jax.experimental.pallas import tpu as pltpu
from jax.sharding import Mesh
from jax.sharding import PartitionSpec as P

bf16 = jnp.bfloat16
f32 = jnp.float32
CHUNK = 128
epsilon = 1e-06


def dot2(left, right, ca, cb):
    return lax.dot_general(left, right, (((ca,), (cb,)), ((), ())), preferred_element_type=f32)


def halves(value):
    high = value.astype(bf16)
    return high, (value - high.astype(f32)).astype(bf16)


def one_pass(left, right, ca, cb):
    return dot2(left.astype(bf16), right.astype(bf16), ca, cb)


def three_pass(left, right, ca, cb):
    lh, ll = halves(left)
    rh, rl = halves(right)
    return dot2(lh, rh, ca, cb) + (dot2(lh, rl, ca, cb) + dot2(ll, rh, ca, cb))


def each(func, left, right, ca=1, cb=0):
    return jnp.stack([func(left[i], right[i], ca, cb) for i in range(left.shape[0])])


def ones_product(ones, value):
    high, low = halves(value)
    return jnp.stack(
        [dot2(ones, high[i], 1, 0) + dot2(ones, low[i], 1, 0) for i in range(value.shape[0])]
    )


def triangles():
    row = lax.broadcasted_iota(jnp.int32, (CHUNK, CHUNK), 0)
    col = lax.broadcasted_iota(jnp.int32, (CHUNK, CHUNK), 1)
    return row, col


def unit_lower_inverse(strict_part, mul):
    row, col = triangles()
    eye = (row == col).astype(f32)
    joined = (row >> 1) == (col >> 1)
    inverse = eye[None] - jnp.where(joined[None], strict_part, 0.0)
    level = 1
    while (1 << level) < CHUNK:
        across = ((row >> (level + 1)) == (col >> (level + 1))) & ((row >> level) != (col >> level))
        below = jnp.where(across[None], strict_part, 0.0)
        inverse = inverse - each(mul, inverse, each(mul, below, inverse))
        level += 1
    return inverse


def decay_factors(logs):
    row, col = triangles()
    lower = (row >= col).astype(bf16)
    total = ones_product(lower, logs)
    middle = total[:, CHUNK // 2 - 1 : CHUNK // 2, :]
    final = total[:, CHUNK - 1 :, :]
    return (
        jnp.exp(total),
        jnp.exp(total - middle),
        jnp.exp(middle - total),
        jnp.exp(final - total),
        jnp.exp(final),
    )


def normalized(values):
    scale = lax.rsqrt(jnp.sum(values * values, axis=-1, keepdims=True) + epsilon)
    return values * scale, scale


def sigmoid(value):
    return 1.0 / (1.0 + jnp.exp(-value))


def chunk_activations(p_ref, up, bias, group, count):
    rows = pl.ds(pl.multiple_of(group * (count * CHUNK), count * CHUNK), count * CHUNK)

    def part(index):
        return p_ref[rows, index * 128 : (index + 1) * 128]

    def blocked(value):
        return value.reshape(count, CHUNK, value.shape[-1])

    queries, q_scale = normalized(part(0))
    key_rows, k_scale = normalized(part(1))
    gate = sigmoid(dot2(part(3).astype(bf16), up, 1, 0) + bias)
    beta = sigmoid(part(4))
    return (
        blocked(queries),
        blocked(key_rows),
        blocked(part(2)),
        blocked(beta),
        blocked(gate),
        blocked(q_scale),
        blocked(k_scale),
    )


def forward_kernel(
    cfg, a_ref, b_ref, w_ref, up_ref, bias_ref,
    mixed_ref, p_ref, x_ref, m_ref, s_ref, t_ref, qe_ref, sv_ref, sk_ref, states_ref,
    off_ref, lo_ref,
):
    mA, mX, mS, mC, count = cfg
    blocks = a_ref.shape[0]
    rows = a_ref.shape[2]

    def project(z, carry):
        total = jnp.zeros((rows, w_ref.shape[-1]), f32)
        for side, ref in ((0, a_ref), (1, b_ref)):
            for x in range(ref.shape[1]):
                total += dot2(ref[z, x], w_ref[side, x], 1, 0)
        p_ref[pl.ds(pl.multiple_of(z * rows, rows), rows), :] = total
        return carry

    lax.fori_loop(0, blocks, project, 0)
    up = up_ref[...]
    bias = bias_ref[...]
    row, col = triangles()
    strict = (row > col)[None]
    lower = (row >= col)[None]
    eye = (row == col)[None]
    chunks = x_ref.shape[0]

    def prepare(group, carry):
        q, k, v, beta, gate, q_scale, k_scale = chunk_activations(p_ref, up, bias, group, count)
        e0, e1, e2, e3, final = decay_factors(-0.25 * gate)
        here = pl.ds(group * count, count)
        key_back = e2 * k
        coupling = jnp.where(strict, each(mA, e1 * k, key_back, 1, 1), 0.0)
        scores = jnp.where(lower, each(mA, e1 * q, key_back, 1, 1), 0.0)
        inverse = unit_lower_inverse(beta * coupling, mX)
        sv = each(mS, inverse, beta * v)
        sk = each(mS, inverse, beta * (e0 * k))
        key_end = e3 * k
        t_ref[here] = jnp.where(eye, final, 0.0) - each(mS, key_end, sk, 0, 0)
        off_ref[here] = each(mS, key_end, sv, 0, 0)
        qe_ref[here] = e0 * q - each(mS, scores, sk)
        lo_ref[here] = each(mS, scores, sv)
        x_ref[here] = inverse
        m_ref[here] = coupling
        s_ref[here] = scores
        sv_ref[here] = sv
        sk_ref[here] = sk
        return carry

    lax.fori_loop(0, chunks // count, prepare, 0)
    state = jnp.zeros((128, 128), f32)
    states_ref[0] = state
    for j in range(chunks - 1):
        state = mC(t_ref[j], state, 1, 0) + off_ref[j]
        states_ref[j + 1] = state
    for j in range(chunks):
        emitted = mS(qe_ref[j], states_ref[j], 1, 0) + lo_ref[j]
        mixed_ref[j * CHUNK : (j + 1) * CHUNK, :] = emitted.astype(bf16)


def backward_kernel(
    cfg, c_ref, d_ref, wo_ref, p_ref, up_ref, bias_ref,
    x_ref, m_ref, s_ref, t_ref, qe_ref, sv_ref, sk_ref, states_ref,
    grad_ref, upg_ref, biasg_ref,
    do_ref, own_ref, ds_ref,
):
    mB, mC, count = cfg
    blocks = c_ref.shape[0]
    rows = c_ref.shape[2]
    chunks = x_ref.shape[0]

    def project(z, carry):
        total = jnp.zeros((rows, 128), f32)
        for side, ref in ((0, c_ref), (1, d_ref)):
            for x in range(ref.shape[1]):
                total += dot2(ref[z, x], wo_ref[side, x], 1, 0)
        per = rows // CHUNK
        do_ref[pl.ds(z * per, per)] = total.reshape(per, CHUNK, 128)
        return carry

    lax.fori_loop(0, blocks, project, 0)
    for j in range(chunks):
        own_ref[j] = mB(qe_ref[j], do_ref[j], 0, 0)
    state = jnp.zeros((128, 128), f32)
    ds_ref[chunks - 1] = state
    for j in range(chunks - 1, 0, -1):
        state = mC(t_ref[j], state, 0, 0) + own_ref[j]
        ds_ref[j - 1] = state
    up = up_ref[...]
    bias = bias_ref[...]
    row, col = triangles()
    strict = (row > col)[None]
    lower = (row >= col)[None]
    upper_ones = (row <= col).astype(bf16)
    upg_ref[...] = jnp.zeros_like(upg_ref)
    biasg_ref[...] = jnp.zeros_like(biasg_ref)

    def finish(group, carry):
        q, k, v, beta, gate, q_scale, k_scale = chunk_activations(p_ref, up, bias, group, count)
        e0, e1, e2, e3, final = decay_factors(-0.25 * gate)
        here = pl.ds(group * count, count)
        d_out = do_ref[here]
        state = states_ref[here]
        d_state = ds_ref[here]
        scores = s_ref[here]
        coupling = m_ref[here]
        key_fwd = e1 * k
        key_back = e2 * k
        query_fwd = e1 * q
        key_start = e0 * k
        key_end = e3 * k
        solved = sv_ref[here] - each(mB, sk_ref[here], state)
        d_solved = each(mB, scores, d_out, 0, 0) + each(mB, key_end, d_state)
        weighted = each(mB, x_ref[here], d_solved, 0, 0)
        d_scores = jnp.where(lower, each(mB, d_out, solved, 1, 1), 0.0)
        d_strict = jnp.where(strict, -each(mB, weighted, solved, 1, 1), 0.0)
        remainder = v - each(mB, key_start, state)
        d_beta = jnp.sum(weighted * remainder, axis=-1, keepdims=True) + jnp.sum(
            d_strict * coupling, axis=-1, keepdims=True
        )
        d_coupling = beta * d_strict
        d_value = beta * weighted
        d_query_start = each(mB, d_out, state, 1, 1)
        d_key_start = -each(mB, d_value, state, 1, 1)
        d_key_end = each(mB, solved, d_state, 1, 1)
        d_key_fwd = each(mB, d_coupling, key_back)
        d_key_back = each(mB, d_coupling, key_fwd, 0, 0) + each(mB, d_scores, query_fwd, 0, 0)
        d_query_fwd = each(mB, d_scores, key_back)
        product = d_state * state
        d_final = jnp.sum(
            jnp.stack([product[i].T for i in range(count)]), axis=1, keepdims=True
        )
        d_query = e1 * d_query_fwd + e0 * d_query_start
        ahead = e1 * d_key_fwd + e0 * d_key_start
        behind = e2 * d_key_back
        ending = e3 * d_key_end
        d_key = ahead + behind + ending
        d_total = q * d_query + k * (ahead - behind - ending)
        last = jnp.sum(k * ending, axis=1, keepdims=True) + final * d_final
        d_log = ones_product(upper_ones, d_total) + last
        d_gate = d_log * (-0.25 * gate * (1.0 - gate))
        d_query = q_scale * (d_query - q * jnp.sum(q * d_query, axis=-1, keepdims=True))
        d_key = k_scale * (d_key - k * jnp.sum(k * d_key, axis=-1, keepdims=True))
        d_logit = d_beta * beta * (1.0 - beta)
        where = pl.ds(pl.multiple_of(group * (count * CHUNK), count * CHUNK), count * CHUNK)
        flat = lambda value: value.reshape(count * CHUNK, 128)
        gate_low = flat(d_gate).astype(bf16)
        grad_ref[where, 0:128] = flat(d_query).astype(bf16)
        grad_ref[where, 128:256] = flat(d_key).astype(bf16)
        grad_ref[where, 256:384] = flat(d_value).astype(bf16)
        grad_ref[where, 384:512] = gate_low
        grad_ref[where, 512:640] = flat(d_logit).astype(bf16)
        upg_ref[...] += dot2(p_ref[where, 384:512].astype(bf16), gate_low, 0, 0)
        biasg_ref[...] += jnp.sum(flat(d_gate), axis=0, keepdims=True)
        return carry

    lax.fori_loop(0, chunks // count, finish, 0)


def vmem(n):
    return [pl.BlockSpec(memory_space=pltpu.VMEM)] * n


def run_forward(a, b, w, up, bias, cfg):
    chunks = a.shape[0] * a.shape[2] // CHUNK
    tokens = chunks * CHUNK
    square = jax.ShapeDtypeStruct((chunks, 128, 128), f32)
    return pl.pallas_call(
        functools.partial(forward_kernel, cfg),
        out_shape=(
            jax.ShapeDtypeStruct((tokens, 128), bf16),
            jax.ShapeDtypeStruct((tokens, 640), f32),
        )
        + (square,) * 8,
        in_specs=vmem(5),
        out_specs=tuple(vmem(10)),
        scratch_shapes=[pltpu.VMEM((chunks, 128, 128), f32)] * 2,
        compiler_params=pltpu.CompilerParams(vmem_limit_bytes=56 << 20),
        name="forward",
    )(a, b, w, up, bias)


def run_backward(c, d, wo, p, up, bias, residuals, cfg):
    chunks = residuals[0].shape[0]
    tokens = chunks * CHUNK
    return pl.pallas_call(
        functools.partial(backward_kernel, cfg),
        out_shape=(
            jax.ShapeDtypeStruct((tokens, 640), bf16),
            jax.ShapeDtypeStruct((128, 128), f32),
            jax.ShapeDtypeStruct((1, 128), f32),
        ),
        in_specs=vmem(6 + len(residuals)),
        out_specs=tuple(vmem(3)),
        scratch_shapes=[pltpu.VMEM((chunks, 128, 128), f32)] * 3,
        compiler_params=pltpu.CompilerParams(vmem_limit_bytes=56 << 20),
        name="backward",
    )(c, d, wo, p, up, bias, *residuals)


def turn(value, axis, by):
    count = lax.axis_size(axis)
    return lax.ppermute(value, axis, [(i, (i + by) % count) for i in range(count)])


def swap(value):
    return lax.ppermute(value, "core", [(0, 1), (1, 0)])


def ordered(own, other, position):
    return jnp.where(position == 0, jnp.stack([own, other]), jnp.stack([other, own]))


def absolute(own, arrived, index):
    ring = [own, arrived[2], arrived[1], arrived[0]]
    return lax.dynamic_slice_in_dim(jnp.stack(ring + ring), 4 - index, 4, axis=0)


def ring_sum(own, arrived):
    wide = [member.astype(f32) for member in [own] + arrived]
    return (wide[0] + wide[2]) + (wide[1] + wide[3])


def scatter_sum(pick, axis):
    index = lax.axis_index(axis)
    arrived = [turn(pick((index + by) % 4), axis, by) for by in (1, 2, 3)]
    return ring_sum(pick(index), arrived)


def shards(
    inputs, output_grad, qkv_weight, out_weight, down_weight, up_weight, beta_weight, gate_bias
):
    z, core, dp, head = (lax.axis_index(name) for name in ("z", "core", "dp", "head"))
    width = qkv_weight.shape[0]
    piece = width // 8
    spot = z * 2 + core

    def gathered(value):
        own = lax.dynamic_slice_in_dim(value, core * piece, piece, axis=1)
        give = lax.dynamic_slice_in_dim(value, (1 - core) * piece, piece, axis=1)
        both = ordered(own, swap(give), core).reshape(-1, piece)
        whole = lax.all_gather(both, ("z", "head"), axis=0, tiled=False)
        whole = whole.reshape((4, 4) + both.shape)
        return whole, swap(whole)

    in_own, in_other = gathered(inputs[0])
    grad_own, grad_other = gathered(output_grad[0])

    def of_head(weight):
        return lax.dynamic_slice_in_dim(weight, spot * 128, 128, axis=weight.ndim - 1)

    def sided(weight):
        blocks = jnp.swapaxes(weight.reshape(4, 2, piece, weight.shape[-1]), 0, 1)
        return jnp.where(core == 0, blocks, blocks[::-1])

    head_weight = of_head(qkv_weight)
    beta_column = lax.dynamic_slice_in_dim(beta_weight, spot, 1, axis=1)
    in_weight = sided(
        jnp.concatenate(
            [head_weight[:, 0], head_weight[:, 1], head_weight[:, 2], down_weight,
             jnp.broadcast_to(beta_column, (width, 128))],
            axis=1,
        )
    )
    back_weight = sided(of_head(out_weight))
    head_up = of_head(up_weight)
    head_bias = of_head(gate_bias)[None]

    mul = three_pass
    mixed, p, *residuals = run_forward(
        in_own, in_other, in_weight, head_up, head_bias, (mul, mul, mul, mul, 4)
    )
    mixed_pair = ordered(mixed, swap(mixed), core)
    grads, up_term, bias_term = run_backward(
        grad_own, grad_other, back_weight, p, head_up, head_bias, residuals, (mul, mul, 4)
    )
    grads_pair = ordered(grads, swap(grads), core)

    def feature_rows(whole):
        return jnp.transpose(whole, (1, 3, 0, 2)).reshape(4 * piece, -1)

    in_rows = feature_rows(in_own)
    grad_rows = feature_rows(grad_own)
    mixed_cols = jnp.concatenate([mixed_pair[0], mixed_pair[1]], axis=1)
    proj_cols = jnp.concatenate(
        [grads_pair[i, :, j * 128 : (j + 1) * 128] for j in range(3) for i in range(2)], axis=1
    )
    out_tile = jnp.dot(grad_rows, mixed_cols, preferred_element_type=f32).astype(bf16)
    proj_tile = jnp.dot(in_rows, proj_cols, preferred_element_type=f32).astype(bf16)
    tile = jnp.concatenate([proj_tile, out_tile], axis=1).reshape(4, 4, piece // 4, 1024)
    summed = scatter_sum(
        lambda at: lax.dynamic_index_in_dim(tile, at, axis=1, keepdims=False), "dp"
    ).astype(bf16)
    moved = lax.all_to_all(summed, "z", 0, 0, tiled=True)
    moved = jnp.transpose(moved.reshape(4, piece // 4, 4, 256), (1, 2, 0, 3))
    moved = moved.reshape(piece // 4, 4, 1024)
    qkv_grad = moved[:, :3]
    out_grad = moved[:, 3]

    pair_up = lax.dynamic_slice_in_dim(up_weight, z * 256, 256, axis=1)
    gate_cols = jnp.concatenate([grads_pair[0, :, 384:512], grads_pair[1, :, 384:512]], axis=1)
    low_pair = jnp.einsum("tc,rc->tr", gate_cols, pair_up, preferred_element_type=f32)
    small_cols = jnp.concatenate(
        [low_pair.astype(bf16), grads_pair[0, :, 512:513], grads_pair[1, :, 512:513]], axis=1
    )
    small_tile = jnp.dot(in_rows, small_cols, preferred_element_type=f32)
    down_tile = small_tile[:, :128].astype(bf16).reshape(4, 4, piece // 4, 128)
    beta_rows = small_tile[:, 128:].T.reshape(-1, 128)
    extra = jnp.concatenate(
        [up_term, beta_rows, bias_term, jnp.zeros((13, 128), f32)], axis=0
    ).astype(bf16)

    def first_pick(at):
        rows = lax.dynamic_index_in_dim(down_tile, at, axis=1, keepdims=False)
        return jnp.concatenate([rows.reshape(piece, 128), extra], axis=0)

    first = scatter_sum(first_pick, "dp").astype(bf16)
    low_rows = first[:piece]
    low_rows = ring_sum(low_rows, [turn(low_rows, "head", by) for by in (1, 2, 3)]).astype(bf16)
    load = jnp.concatenate([low_rows, first[piece:]], axis=0)
    arrived = [turn(load, "z", by) for by in (1, 2, 3)]
    low_rows = ring_sum(load[:piece], [member[:piece] for member in arrived]).astype(bf16)
    extras = absolute(load[piece:], [member[piece:] for member in arrived], z)
    low_all = absolute(low_rows, [turn(low_rows, "dp", by) for by in (1, 2, 3)], dp)
    ready = jnp.concatenate([low_all.reshape(-1, 128), extras.reshape(-1, 128)], axis=0)
    ready = ordered(ready, swap(ready), core)
    down_grad = ready[:, : 4 * piece].reshape(2, 4, 4, piece // 4, 128)
    down_grad = jnp.transpose(down_grad, (2, 0, 1, 3, 4)).reshape(width, 128).astype(f32)
    extras = ready[:, 4 * piece :].reshape(2, 4, -1, 128).astype(f32)
    up_grad = jnp.transpose(extras[:, :, :128], (2, 1, 0, 3)).reshape(128, 1024)
    beta_grad = extras[:, :, 128:146].reshape(2, 4, 2, 4, piece)
    beta_grad = jnp.transpose(beta_grad, (3, 0, 4, 1, 2)).reshape(width, 8)
    bias_grad = jnp.transpose(extras[:, :, 146], (1, 0, 2)).reshape(1024)

    def to_tokens(pair):
        cut = pair.reshape(2, 4, 2, 128, pair.shape[-1])
        cut = lax.dynamic_index_in_dim(cut, core, axis=2, keepdims=False)
        cut = jnp.swapaxes(cut, 0, 1)
        back = lax.all_to_all(cut, "z", 0, 0, tiled=True)
        return jnp.swapaxes(back.reshape(8, 128, pair.shape[-1]), 0, 1)

    def head_share(part):
        share = part.astype(bf16)
        return scatter_sum(
            lambda at: lax.dynamic_slice_in_dim(share, at * 2 * piece, 2 * piece, axis=1), "head"
        ).astype(bf16)[None]

    mixed_tokens = to_tokens(mixed_pair).reshape(128, 1024)
    layer_out = head_share(
        jnp.einsum("tc,dc->td", mixed_tokens, out_weight, preferred_element_type=f32)
    )
    tokens = to_tokens(grads_pair)
    proj_low = jnp.concatenate(
        [tokens[:, :, j * 128 : (j + 1) * 128].reshape(128, 1024) for j in range(3)], axis=1
    )
    gate_low = tokens[:, :, 384:512].reshape(128, 1024)
    logit_low = tokens[:, :, 512]
    low_grad = jnp.einsum("tc,rc->tr", gate_low, up_weight, preferred_element_type=f32)
    part = jnp.einsum(
        "tc,dc->td", proj_low, qkv_weight.reshape(width, 3072), preferred_element_type=f32
    )
    part = part + jnp.einsum(
        "tr,dr->td", low_grad.astype(bf16), down_weight, preferred_element_type=f32
    )
    part = part + jnp.einsum("th,dh->td", logit_low, beta_weight, preferred_element_type=f32)
    input_grad = head_share(part)
    return (layer_out, input_grad, qkv_grad, out_grad, up_grad, down_grad, beta_grad, bias_grad)


def solution(mesh):
    fine = Mesh(
        mesh.devices.reshape(4, 2, mesh.shape["dp"], mesh.shape["head"]),
        ("z", "core", "dp", "head"),
    )
    context = ("z", "core")
    return jax.shard_map(
        shards,
        mesh=fine,
        in_specs=(
            P("dp", context, "head"),
            P("dp", context, "head"),
            P(None, None, "head"),
            P(None, "head"),
            P(),
            P(None, "head"),
            P(None, "head"),
            P("head"),
        ),
        out_specs=(
            P("dp", context, "head"),
            P("dp", context, "head"),
            P(context + ("dp",), None, "head"),
            P(context + ("dp",), "head"),
            P(None, "head"),
            P(),
            P(None, "head"),
            P("head"),
        ),
        check_vma=False,
    )
```

```python
import functools
import jax
import jax.numpy as jnp
from jax import lax
from jax.experimental import pallas as pl
from jax.experimental.pallas import tpu as pltpu
from jax.sharding import Mesh
from jax.sharding import PartitionSpec as P

bf16 = jnp.bfloat16
f32 = jnp.float32
CHUNK = 128
epsilon = 1e-06


def dot2(left, right, ca, cb):
    return lax.dot_general(left, right, (((ca,), (cb,)), ((), ())), preferred_element_type=f32)


def halves(value):
    high = value.astype(bf16)
    return high, (value - high.astype(f32)).astype(bf16)


def one_pass(left, right, ca, cb):
    return dot2(left.astype(bf16), right.astype(bf16), ca, cb)


def three_pass(left, right, ca, cb):
    lh, ll = halves(left)
    rh, rl = halves(right)
    return dot2(lh, rh, ca, cb) + (dot2(lh, rl, ca, cb) + dot2(ll, rh, ca, cb))


def each(func, left, right, ca=1, cb=0):
    return jnp.stack([func(left[i], right[i], ca, cb) for i in range(left.shape[0])])


def ones_product(ones, value):
    high, low = halves(value)
    return jnp.stack(
        [dot2(ones, high[i], 1, 0) + dot2(ones, low[i], 1, 0) for i in range(value.shape[0])]
    )


def triangles():
    row = lax.broadcasted_iota(jnp.int32, (CHUNK, CHUNK), 0)
    col = lax.broadcasted_iota(jnp.int32, (CHUNK, CHUNK), 1)
    return row, col


def unit_lower_inverse(strict_part, mul):
    row, col = triangles()
    eye = (row == col).astype(f32)
    joined = (row >> 1) == (col >> 1)
    inverse = eye[None] - jnp.where(joined[None], strict_part, 0.0)
    level = 1
    while (1 << level) < CHUNK:
        across = ((row >> (level + 1)) == (col >> (level + 1))) & ((row >> level) != (col >> level))
        below = jnp.where(across[None], strict_part, 0.0)
        inverse = inverse - each(mul, inverse, each(mul, below, inverse))
        level += 1
    return inverse


def decay_factors(logs):
    row, col = triangles()
    lower = (row >= col).astype(bf16)
    total = ones_product(lower, logs)
    middle = total[:, CHUNK // 2 - 1 : CHUNK // 2, :]
    final = total[:, CHUNK - 1 :, :]
    return (
        jnp.exp(total),
        jnp.exp(total - middle),
        jnp.exp(middle - total),
        jnp.exp(final - total),
        jnp.exp(final),
    )


def normalized(values):
    scale = lax.rsqrt(jnp.sum(values * values, axis=-1, keepdims=True) + epsilon)
    return values * scale, scale


def sigmoid(value):
    return 1.0 / (1.0 + jnp.exp(-value))


def chunk_activations(p_ref, up, bias, group, count):
    rows = pl.ds(pl.multiple_of(group * (count * CHUNK), count * CHUNK), count * CHUNK)

    def part(index):
        return p_ref[rows, index * 128 : (index + 1) * 128]

    def blocked(value):
        return value.reshape(count, CHUNK, value.shape[-1])

    queries, q_scale = normalized(part(0))
    key_rows, k_scale = normalized(part(1))
    gate = sigmoid(dot2(part(3).astype(bf16), up, 1, 0) + bias)
    beta = sigmoid(part(4))
    return (
        blocked(queries),
        blocked(key_rows),
        blocked(part(2)),
        blocked(beta),
        blocked(gate),
        blocked(q_scale),
        blocked(k_scale),
    )


def start_all(copies):
    for copy in copies:
        copy.start()
    return copies


def wait_all(copies):
    for copy in copies:
        copy.wait()


def piece_copies(out_ref, early_refs, late_refs, side, array, at, sem):
    z, core, head = at[0], at[1], at[3]
    copies = []
    for own_tokens in (True, False):
        token_core = core if own_tokens == (side == 0) else 1 - core
        for first in range(4):
            for second in range(4):
                dx, dz = (first, second) if own_tokens else (second, first)
                if first == 0:
                    piece = early_refs[0 if own_tokens else 1].at[second, array]
                else:
                    piece = late_refs[first - 1 + (0 if own_tokens else 3)].at[second, array]
                block = lax.rem(z + (4 - dz), 4) * 2 + token_core
                lanes = pl.ds(pl.multiple_of(block * 128, 128), 128)
                place = out_ref.at[side, lax.rem(head + (4 - dx), 4), :, lanes]
                copies.append(pltpu.make_async_copy(piece, place, sem))
    return copies


def from_features(in_ref, w_ref, core, tokens):
    total = None
    for side in range(2):
        half = core if side == 0 else 1 - core
        for x in range(4):
            term = dot2(in_ref[side, x, :, tokens], w_ref[x, half], 0, 0)
            total = term if total is None else total + term
    return total


def recurrence_kernel(
    mul, count, at_ref, *refs,
):
    pieces, refs = refs[:16], refs[16:]
    (
        w_ref, wo_ref, up_ref, bias_ref,
        tile0_ref, tile1_ref, tile2_ref, tile3_ref, all_ref, keep_ref, give_ref, extra_ref,
        in_ref, grad_in_ref, p_ref, x_ref, m_ref, s_ref, t_ref, qe_ref, sv_ref, sk_ref,
        states_ref, off_ref, do_ref, own_ref, ds_ref, right_ref, rows_ref, logit_ref,
        in_sem, grad_sem,
    ) = refs
    mA = mX = mS = mC = mB = mul
    lo_ref = own_ref
    mixed_ref = all_ref.at[:, 640:768]
    at = [at_ref[i] for i in range(4)]
    core, dp = at[1], at[2]
    sides = ((pieces[:2], pieces[2:8]), (pieces[8:10], pieces[10:16]))
    flights = [
        start_all(
            [
                copy
                for side in range(2)
                for copy in piece_copies(out_ref, *sides[side], side, array, at, sem)
            ]
        )
        for array, (out_ref, sem) in enumerate(((in_ref, in_sem), (grad_in_ref, grad_sem)))
    ]
    wait_all(flights[0])
    for block in range(4):
        rows = slice(block * 256, (block + 1) * 256)
        p_ref[rows, :] = from_features(in_ref, w_ref, core, rows)
    up = up_ref[...]
    bias = bias_ref[...]
    row, col = triangles()
    strict = (row > col)[None]
    lower = (row >= col)[None]
    eye = (row == col)[None]
    chunks = x_ref.shape[0]

    def prepare(group, carry):
        q, k, v, beta, gate, q_scale, k_scale = chunk_activations(p_ref, up, bias, group, count)
        e0, e1, e2, e3, final = decay_factors(-0.25 * gate)
        here = pl.ds(group * count, count)
        key_back = e2 * k
        coupling = jnp.where(strict, each(mA, e1 * k, key_back, 1, 1), 0.0)
        scores = jnp.where(lower, each(mA, e1 * q, key_back, 1, 1), 0.0)
        inverse = unit_lower_inverse(beta * coupling, mX)
        sv = each(mS, inverse, beta * v)
        sk = each(mS, inverse, beta * (e0 * k))
        key_end = e3 * k
        t_ref[here] = jnp.where(eye, final, 0.0) - each(mS, key_end, sk, 0, 0)
        off_ref[here] = each(mS, key_end, sv, 0, 0)
        qe_ref[here] = e0 * q - each(mS, scores, sk)
        lo_ref[here] = each(mS, scores, sv)
        x_ref[here] = inverse
        m_ref[here] = coupling
        s_ref[here] = scores
        sv_ref[here] = sv
        sk_ref[here] = sk
        return carry

    lax.fori_loop(0, chunks // count, prepare, 0)
    state = jnp.zeros((128, 128), f32)
    states_ref[0] = state
    for j in range(chunks - 1):
        state = mC(t_ref[j], state, 1, 0) + off_ref[j]
        states_ref[j + 1] = state
    for j in range(chunks):
        emitted = mS(qe_ref[j], states_ref[j], 1, 0) + lo_ref[j]
        mixed_ref[j * CHUNK : (j + 1) * CHUNK, :] = emitted.astype(bf16)


    wait_all(flights[1])
    for block in range(4):
        rows = slice(block * 256, (block + 1) * 256)
        do_ref[2 * block : 2 * block + 2] = from_features(grad_in_ref, wo_ref, core, rows).reshape(
            2, CHUNK, 128
        )
    for j in range(chunks):
        own_ref[j] = mB(qe_ref[j], do_ref[j], 0, 0)
    state = jnp.zeros((128, 128), f32)
    ds_ref[chunks - 1] = state
    for j in range(chunks - 1, 0, -1):
        state = mC(t_ref[j], state, 0, 0) + own_ref[j]
        ds_ref[j - 1] = state
    upper_ones = (row <= col).astype(bf16)
    extra_ref[...] = jnp.zeros_like(extra_ref)

    def finish(group, carry):
        q, k, v, beta, gate, q_scale, k_scale = chunk_activations(p_ref, up, bias, group, count)
        e0, e1, e2, e3, final = decay_factors(-0.25 * gate)
        here = pl.ds(group * count, count)
        d_out = do_ref[here]
        state = states_ref[here]
        d_state = ds_ref[here]
        scores = s_ref[here]
        coupling = m_ref[here]
        key_fwd = e1 * k
        key_back = e2 * k
        query_fwd = e1 * q
        key_start = e0 * k
        key_end = e3 * k
        solved = sv_ref[here] - each(mB, sk_ref[here], state)
        d_solved = each(mB, scores, d_out, 0, 0) + each(mB, key_end, d_state)
        weighted = each(mB, x_ref[here], d_solved, 0, 0)
        d_scores = jnp.where(lower, each(mB, d_out, solved, 1, 1), 0.0)
        d_strict = jnp.where(strict, -each(mB, weighted, solved, 1, 1), 0.0)
        remainder = v - each(mB, key_start, state)
        d_beta = jnp.sum(weighted * remainder, axis=-1, keepdims=True) + jnp.sum(
            d_strict * coupling, axis=-1, keepdims=True
        )
        d_coupling = beta * d_strict
        d_value = beta * weighted
        d_query_start = each(mB, d_out, state, 1, 1)
        d_key_start = -each(mB, d_value, state, 1, 1)
        d_key_end = each(mB, solved, d_state, 1, 1)
        d_key_fwd = each(mB, d_coupling, key_back)
        d_key_back = each(mB, d_coupling, key_fwd, 0, 0) + each(mB, d_scores, query_fwd, 0, 0)
        d_query_fwd = each(mB, d_scores, key_back)
        product = d_state * state
        d_final = jnp.sum(
            jnp.stack([product[i].T for i in range(count)]), axis=1, keepdims=True
        )
        d_query = e1 * d_query_fwd + e0 * d_query_start
        ahead = e1 * d_key_fwd + e0 * d_key_start
        behind = e2 * d_key_back
        ending = e3 * d_key_end
        d_key = ahead + behind + ending
        d_total = q * d_query + k * (ahead - behind - ending)
        last = jnp.sum(k * ending, axis=1, keepdims=True) + final * d_final
        d_log = ones_product(upper_ones, d_total) + last
        d_gate = d_log * (-0.25 * gate * (1.0 - gate))
        d_query = q_scale * (d_query - q * jnp.sum(q * d_query, axis=-1, keepdims=True))
        d_key = k_scale * (d_key - k * jnp.sum(k * d_key, axis=-1, keepdims=True))
        d_logit = d_beta * beta * (1.0 - beta)
        where = pl.ds(pl.multiple_of(group * (count * CHUNK), count * CHUNK), count * CHUNK)
        flat = lambda value: value.reshape(count * CHUNK, 128)
        gate_low = flat(d_gate).astype(bf16)
        parts = [
            flat(d_query).astype(bf16),
            flat(d_key).astype(bf16),
            flat(d_value).astype(bf16),
            gate_low,
            flat(d_logit).astype(bf16),
        ]
        for index, part in enumerate(parts):
            lanes = slice(index * 128, (index + 1) * 128)
            all_ref[where, lanes] = part
            if index == 3:
                right_ref[where, lanes] = dot2(gate_low, up, 1, 1).astype(bf16)
            elif index < 3:
                right_ref[where, lanes] = part
        for i in range(count):
            lanes = pl.ds(pl.multiple_of((group * count + i) * CHUNK, CHUNK), CHUNK)
            logit_ref[:, lanes] = d_logit[i].T[0:16].astype(bf16)
        extra_ref[0:128, :] += dot2(p_ref[where, 384:512].astype(bf16), gate_low, 0, 0)
        extra_ref[128:129, :] += jnp.sum(flat(d_gate), axis=0, keepdims=True)
        return carry

    lax.fori_loop(0, chunks // count, finish, 0)
    for side in range(2):
        half = core if side == 0 else 1 - core
        for x in range(4):
            piece = dot2(in_ref[side, x], right_ref[...], 1, 0)
            rows_ref[:, 0:384] = piece[:, 0:384]
            rows_ref[:, 384:512] = dot2(grad_in_ref[side, x], mixed_ref[...], 1, 0)
            (keep_ref if side == 0 else give_ref)[x] = piece[:, 384:512].astype(bf16)
            beta = dot2(logit_ref[...], in_ref[side, x], 1, 1)
            first = 136 + (x * 2 + half) * 3
            extra_ref[pl.ds(first, 1), :] = beta[0:1, 0:128]
            extra_ref[pl.ds(first + 1, 1), :] = beta[0:1, 128:256]
            extra_ref[pl.ds(first + 2, 1), 0:32] = beta[0:1, 256:288]
            for by, ref in enumerate((tile0_ref, tile1_ref, tile2_ref, tile3_ref)):
                start = lax.rem(dp + by, 4) * 72
                ref[x, half] = rows_ref[pl.ds(pl.multiple_of(start, 8), 72), :].astype(bf16)


TOKENS = 128


def output_kernel(
    at_ref, heads_ref, w_ref, wo_ref, down_ref, up_ref, beta_ref,
    out0_ref, out1_ref, out2_ref, out3_ref,
    left_ref, low_ref,
):
    step = pl.program_id(0)
    block = out0_ref.shape[1] // 2

    @pl.when(step == 0)
    def prepare():
        lane = lax.broadcasted_iota(jnp.int32, (TOKENS, 128), 1)
        logits = jnp.zeros((TOKENS, 128), f32)
        for h in range(8):
            lanes = slice(h * 128, (h + 1) * 128)
            for index, part in enumerate((0, 1, 2, 5, 3)):
                left_ref[index, :, lanes] = heads_ref[h, :, part * 128 : (part + 1) * 128]
            logits = logits + jnp.where(lane == h, heads_ref[h, :, 512:640].astype(f32), 0.0)
        low_ref[0] = dot2(left_ref[4], up_ref[...], 1, 1).astype(bf16)
        low_ref[1] = logits.astype(bf16)

    share = dot2(wo_ref[...], left_ref[3], 1, 1)
    part = dot2(w_ref[0], left_ref[0], 1, 1)
    part += dot2(w_ref[1], left_ref[1], 1, 1)
    part += dot2(w_ref[2], left_ref[2], 1, 1)
    part += dot2(down_ref[...], low_ref[0], 1, 1)
    part += dot2(beta_ref[...], low_ref[1], 1, 1)
    for by, ref in enumerate((out0_ref, out1_ref, out2_ref, out3_ref)):

        for half in range(2):

            @pl.when(step == 2 * by + half)
            def store(ref=ref, rows=slice(half * block, (half + 1) * block)):
                ref[0, rows] = share.astype(bf16)
                ref[1, rows] = part.astype(bf16)


def small_kernel(at_ref, own_ref, other_ref, down_ref, up_ref, bias_ref, beta_ref):
    z, core, dp = at_ref[0], at_ref[1], at_ref[2]
    for side, ref in enumerate((own_ref, other_ref)):
        half = core if side == 0 else 1 - core
        for i in range(4):
            low = ref[i * 288 : (i + 1) * 288, :].astype(f32)
            place = lax.rem(dp + (4 - i), 4)
            for zp in range(4):
                down_ref[zp, half, place] = low[zp * 72 : (zp + 1) * 72]
            extra = ref[1152 + i * 160 : 1152 + (i + 1) * 160, :].astype(f32)
            head = lax.rem(z + (4 - i), 4) * 2 + half
            up_ref[:, pl.ds(pl.multiple_of(head * 128, 128), 128)] = extra[0:128]
            bias_ref[pl.ds(head, 1), :] = extra[128:129]
            beta_ref[head] = extra[136:160]


def place_kernel(in_ref, qkv_ref, out_ref):
    for h in range(8):
        lanes = slice(h * 128, (h + 1) * 128)
        for j in range(3):
            qkv_ref[j, :, lanes] = in_ref[h, :, j * 128 : (j + 1) * 128]
        out_ref[:, lanes] = in_ref[h, :, 384:512]


def vmem(n):
    return [pl.BlockSpec(memory_space=pltpu.VMEM)] * n


def anywhere(n):
    return [pl.BlockSpec(memory_space=pl.ANY)] * n


def cost(flops, bytes_accessed):
    return pl.CostEstimate(flops=flops, bytes_accessed=bytes_accessed, transcendentals=0)


def run_recurrence(at, pieces, w, wo, up, bias):
    chunks, tokens = 8, 1024
    shape = jax.ShapeDtypeStruct
    return pl.pallas_call(
        functools.partial(recurrence_kernel, three_pass, 4),
        out_shape=(shape((4, 2, 72, 512), bf16),) * 4
        + (shape((tokens, 768), bf16),)
        + (shape((4, 288, 128), bf16),) * 2
        + (shape((160, 128), f32),),
        in_specs=[pl.BlockSpec(memory_space=pltpu.SMEM)] + anywhere(len(pieces)) + vmem(4),
        out_specs=tuple(vmem(8)),
        scratch_shapes=[pltpu.VMEM((2, 4, 288, tokens), bf16)] * 2
        + [pltpu.VMEM((tokens, 640), f32)]
        + [pltpu.VMEM((chunks, 128, 128), f32)] * 12
        + [
            pltpu.VMEM((tokens, 512), bf16),
            pltpu.VMEM((288, 512), f32),
            pltpu.VMEM((16, tokens), bf16),
            pltpu.SemaphoreType.DMA,
            pltpu.SemaphoreType.DMA,
        ],
        compiler_params=pltpu.CompilerParams(vmem_limit_bytes=52 << 20),
        cost_estimate=cost(16_000_000_000, 40_000_000),
        name="recurrence",
    )(at, *pieces, w, wo, up, bias)


def run_output(at, heads, w, wo, down, up, beta):
    block = w.shape[1] // 8

    def rows(step, at_ref):
        return (lax.rem(at_ref[3] * 2 + step, 8), 0)

    def deep_rows(step, at_ref):
        return (0, lax.rem(at_ref[3] * 2 + step, 8), 0)

    whole = lambda value: pl.BlockSpec(value.shape, lambda step, at_ref: (0,) * len(value.shape))
    out = jax.ShapeDtypeStruct((2, 2 * block, TOKENS), bf16)
    return pl.pallas_call(
        output_kernel,
        out_shape=(out,) * 4,
        grid_spec=pltpu.PrefetchScalarGridSpec(
            num_scalar_prefetch=1,
            grid=(8,),
            in_specs=[
                whole(heads),
                pl.BlockSpec((3, block, w.shape[2]), deep_rows),
                pl.BlockSpec((block, wo.shape[1]), rows),
                pl.BlockSpec((block, down.shape[1]), rows),
                whole(up),
                pl.BlockSpec((block, beta.shape[1]), rows),
            ],
            out_specs=tuple([whole(out)] * 4),
            scratch_shapes=[
                pltpu.VMEM((5, TOKENS, 1024), bf16),
                pltpu.VMEM((2, TOKENS, 128), bf16),
            ],
        ),
        compiler_params=pltpu.CompilerParams(vmem_limit_bytes=48 << 20),
        cost_estimate=cost(3_000_000_000, 20_000_000),
        name="output",
    )(at, heads, w, wo, down, up, beta)


def run_small(at, own, other):
    shape = jax.ShapeDtypeStruct
    return pl.pallas_call(
        small_kernel,
        out_shape=(
            shape((4, 2, 4, 72, 128), f32),
            shape((128, 1024), f32),
            shape((8, 128), f32),
            shape((8, 24, 128), f32),
        ),
        in_specs=[pl.BlockSpec(memory_space=pltpu.SMEM)] + vmem(2),
        out_specs=tuple(vmem(4)),
        cost_estimate=cost(1_000_000, 4_000_000),
        name="small",
    )(at, own, other)


def run_place(moved):
    rows = moved.shape[1]
    return pl.pallas_call(
        place_kernel,
        out_shape=(
            jax.ShapeDtypeStruct((3, rows, 1024), bf16),
            jax.ShapeDtypeStruct((rows, 1024), bf16),
        ),
        in_specs=vmem(1),
        out_specs=tuple(vmem(2)),
        cost_estimate=cost(1_000_000, 1_200_000),
        name="place",
    )(moved)


def turn(value, axis, by):
    count = lax.axis_size(axis)
    return lax.ppermute(value, axis, [(i, (i + by) % count) for i in range(count)])


def swap(value):
    return lax.ppermute(value, "core", [(0, 1), (1, 0)])


def selector(value, count):
    return lax.broadcasted_iota(jnp.int32, (count,) + (1,) * value.ndim, 0)


def ordered(own, other, position):
    return jnp.where(selector(own, 2) == position, own[None], other[None])


def stacked(members):
    at = selector(members[0], 4)
    low = jnp.where(at == 0, members[0][None], members[1][None])
    high = jnp.where(at == 2, members[2][None], members[3][None])
    return jnp.where(at < 2, low, high)


def ring_sum(own, arrived):
    wide = [member.astype(f32) for member in [own] + arrived]
    return (wide[0] + wide[2]) + (wide[1] + wide[3])


def scatter_sum(pick, axis):
    index = lax.axis_index(axis)
    arrived = [turn(pick((index + by) % 4), axis, by) for by in (1, 2, 3)]
    return ring_sum(pick(index), arrived)


def shards(
    inputs, output_grad, qkv_weight, out_weight, down_weight, up_weight, beta_weight, gate_bias
):
    z, core, dp, head = (lax.axis_index(name) for name in ("z", "core", "dp", "head"))
    at = jnp.stack([z, core, dp, head]).astype(jnp.int32)
    width = qkv_weight.shape[0]
    piece = width // 8
    spot = z * 2 + core
    steps = (1, 2, 3)

    both = jnp.stack([inputs[0].T, output_grad[0].T])
    own = lax.dynamic_slice_in_dim(both, core * piece, piece, axis=1)
    got = swap(lax.dynamic_slice_in_dim(both, (1 - core) * piece, piece, axis=1))

    early = [
        stacked([own] + [turn(own, "z", by) for by in steps]),
        stacked([got] + [turn(got, "head", by) for by in steps]),
    ]
    late = [turn(early[0], "head", by) for by in steps]
    late += [turn(early[1], "z", by) for by in steps]
    pieces = early + late
    pieces += [swap(member) for member in pieces]

    def of_head(weight):
        return lax.dynamic_slice_in_dim(weight, spot * 128, 128, axis=weight.ndim - 1)

    def blocked(weight):
        return weight.reshape(4, 2, piece, weight.shape[-1])

    head_weight = of_head(qkv_weight)
    beta_column = lax.dynamic_slice_in_dim(beta_weight, spot, 1, axis=1)
    in_weight = blocked(
        jnp.concatenate(
            [head_weight[:, 0], head_weight[:, 1], head_weight[:, 2], down_weight,
             jnp.broadcast_to(beta_column, (width, 128))],
            axis=1,
        )
    )
    back_weight = blocked(of_head(out_weight))
    head_up = of_head(up_weight)
    head_bias = of_head(gate_bias)[None]

    outs = run_recurrence(at, pieces, in_weight, back_weight, head_up, head_bias)
    tiles, (tokens, down_keep, down_give, extra) = outs[:4], outs[4:]

    arrived = [turn(tiles[by], "dp", by) for by in steps]
    heads = lax.all_to_all(tokens.reshape(8, 128, 768), ("z", "core"), 0, 0, tiled=True)
    down_got = swap(down_give)

    down_tile = (down_keep.astype(f32) + down_got.astype(f32)).astype(bf16)
    down_tile = down_tile.reshape(4, 4, piece // 4, 128)
    extra = extra.astype(bf16)

    def first_pick(index):
        rows = lax.dynamic_index_in_dim(down_tile, index, axis=1, keepdims=False)
        return jnp.concatenate([rows.reshape(piece, 128), extra], axis=0)

    first = scatter_sum(first_pick, "dp").astype(bf16)
    low_rows = first[:piece]
    low_rows = ring_sum(low_rows, [turn(low_rows, "head", by) for by in steps]).astype(bf16)
    load = jnp.concatenate([low_rows, first[piece:]], axis=0)
    came = [turn(load, "z", by) for by in steps]
    low_rows = ring_sum(load[:piece], [member[:piece] for member in came]).astype(bf16)
    low_all = [low_rows] + [turn(low_rows, "dp", by) for by in steps]
    ready = jnp.concatenate(low_all + [member[piece:] for member in [load] + came], axis=0)
    down_grad, up_grad, bias_grad, beta_grad = run_small(at, ready, swap(ready))
    down_grad = down_grad.reshape(width, 128)
    bias_grad = bias_grad.reshape(1024)
    beta_grad = beta_grad.reshape(8, 8, 384)[:, :, :piece].reshape(8, width).T

    arrived, heads = lax.optimization_barrier((arrived, heads))
    shares = run_output(
        at, heads, jnp.swapaxes(qkv_weight, 0, 1), out_weight, down_weight, up_weight,
        jnp.pad(beta_weight, ((0, 0), (0, 120))),
    )
    results = ring_sum(shares[0], [turn(shares[by], "head", by) for by in steps]).astype(bf16)
    layer_out = results[0].T[None]
    input_grad = results[1].T[None]

    summed = ring_sum(tiles[0], arrived).astype(bf16)
    moved = lax.all_to_all(
        summed.reshape(8, piece // 4, 512), ("z", "core"), 0, 0, tiled=True
    )
    qkv_grad, out_grad = run_place(moved)
    qkv_grad = jnp.swapaxes(qkv_grad, 0, 1)
    return (layer_out, input_grad, qkv_grad, out_grad, up_grad, down_grad, beta_grad, bias_grad)


def solution(mesh):
    fine = Mesh(
        mesh.devices.reshape(4, 2, mesh.shape["dp"], mesh.shape["head"]),
        ("z", "core", "dp", "head"),
    )
    context = ("z", "core")
    return jax.shard_map(
        shards,
        mesh=fine,
        in_specs=(
            P("dp", context, "head"),
            P("dp", context, "head"),
            P(None, None, "head"),
            P(None, "head"),
            P(),
            P(None, "head"),
            P(None, "head"),
            P("head"),
        ),
        out_specs=(
            P("dp", context, "head"),
            P("dp", context, "head"),
            P(context + ("dp",), None, "head"),
            P(context + ("dp",), "head"),
            P(None, "head"),
            P(),
            P(None, "head"),
            P("head"),
        ),
        check_vma=False,
    )
```

```python
import functools
import jax
import jax.numpy as jnp
from jax import lax
from jax.experimental import pallas as pl
from jax.experimental.pallas import tpu as pltpu
from jax.sharding import Mesh
from jax.sharding import PartitionSpec as P

bf16 = jnp.bfloat16
f32 = jnp.float32
CHUNK = 128
epsilon = 1e-06


def dot2(left, right, ca, cb):
    return lax.dot_general(left, right, (((ca,), (cb,)), ((), ())), preferred_element_type=f32)


def halves(value):
    high = value.astype(bf16)
    return high, (value - high.astype(f32)).astype(bf16)


def one_pass(left, right, ca, cb):
    return dot2(left.astype(bf16), right.astype(bf16), ca, cb)


def three_pass(left, right, ca, cb):
    lh, ll = halves(left)
    rh, rl = halves(right)
    return dot2(lh, rh, ca, cb) + (dot2(lh, rl, ca, cb) + dot2(ll, rh, ca, cb))


def each(func, left, right, ca=1, cb=0):
    return jnp.stack([func(left[i], right[i], ca, cb) for i in range(left.shape[0])])


def ones_product(ones, value):
    high, low = halves(value)
    return jnp.stack(
        [dot2(ones, high[i], 1, 0) + dot2(ones, low[i], 1, 0) for i in range(value.shape[0])]
    )


def triangles():
    row = lax.broadcasted_iota(jnp.int32, (CHUNK, CHUNK), 0)
    col = lax.broadcasted_iota(jnp.int32, (CHUNK, CHUNK), 1)
    return row, col


def unit_lower_inverse(strict_part, mul):
    row, col = triangles()
    eye = (row == col).astype(f32)
    joined = (row >> 1) == (col >> 1)
    inverse = eye[None] - jnp.where(joined[None], strict_part, 0.0)
    level = 1
    while (1 << level) < CHUNK:
        across = ((row >> (level + 1)) == (col >> (level + 1))) & ((row >> level) != (col >> level))
        below = jnp.where(across[None], strict_part, 0.0)
        inverse = inverse - each(mul, inverse, each(mul, below, inverse))
        level += 1
    return inverse


def decay_factors(logs):
    row, col = triangles()
    lower = (row >= col).astype(bf16)
    total = ones_product(lower, logs)
    middle = total[:, CHUNK // 2 - 1 : CHUNK // 2, :]
    final = total[:, CHUNK - 1 :, :]
    return (
        jnp.exp(total),
        jnp.exp(total - middle),
        jnp.exp(middle - total),
        jnp.exp(final - total),
        jnp.exp(final),
    )


def normalized(values):
    scale = lax.rsqrt(jnp.sum(values * values, axis=-1, keepdims=True) + epsilon)
    return values * scale, scale


def sigmoid(value):
    return 1.0 / (1.0 + jnp.exp(-value))


def chunk_activations(p_ref, up, bias, group, count):
    rows = pl.ds(pl.multiple_of(group * (count * CHUNK), count * CHUNK), count * CHUNK)

    def part(index):
        return p_ref[rows, index * 128 : (index + 1) * 128]

    def blocked(value):
        return value.reshape(count, CHUNK, value.shape[-1])

    queries, q_scale = normalized(part(0))
    key_rows, k_scale = normalized(part(1))
    gate = sigmoid(dot2(part(3).astype(bf16), up, 1, 0) + bias)
    beta = sigmoid(part(4))
    return (
        blocked(queries),
        blocked(key_rows),
        blocked(part(2)),
        blocked(beta),
        blocked(gate),
        blocked(q_scale),
        blocked(k_scale),
    )


def start_all(copies):
    for copy in copies:
        copy.start()
    return copies


def wait_all(copies):
    for copy in copies:
        copy.wait()


def piece_copies(out_ref, early_refs, late_refs, side, array, at, sem):
    z, core, head = at[0], at[1], at[3]
    copies = []
    for own_tokens in (True, False):
        token_core = core if own_tokens == (side == 0) else 1 - core
        for first in range(4):
            for second in range(4):
                dx, dz = (first, second) if own_tokens else (second, first)
                if first == 0:
                    piece = early_refs[0 if own_tokens else 1].at[second, array]
                else:
                    piece = late_refs[first - 1 + (0 if own_tokens else 3)].at[second, array]
                block = lax.rem(z + (4 - dz), 4) * 2 + token_core
                lanes = pl.ds(pl.multiple_of(block * 128, 128), 128)
                half = core if side == 0 else 1 - core
                first_row = (lax.rem(head + (4 - dx), 4) * 2 + half) * 288
                place = out_ref.at[pl.ds(pl.multiple_of(first_row, 16), 288), lanes]
                copies.append(pltpu.make_async_copy(piece, place, sem))
    return copies


def recurrence_kernel(
    mul, count, at_ref, *refs,
):
    pieces, refs = refs[:16], refs[16:]
    (
        qkv_ref, out_ref, down_ref, beta_ref, all_up_ref, all_bias_ref,
        tile_ref, tokens_ref, keep_ref, give_ref, extra_ref,
        mixed_ref, in_ref, grad_in_ref, p_ref, x_ref, m_ref, s_ref, t_ref, qe_ref, sv_ref, sk_ref,
        states_ref, off_ref, do_ref, own_ref, ds_ref, right_ref, rows_ref, logit_ref,
        w_ref, wo_ref, up_ref, in_sem, grad_sem, w_sem,
    ) = refs
    mA = mX = mS = mC = mB = mul
    lo_ref = own_ref
    at = [at_ref[i] for i in range(4)]
    core = at[1]
    own_lanes = pl.ds(pl.multiple_of((at[0] * 2 + core) * 128, 128), 128)
    weights = start_all(
        [
            pltpu.make_async_copy(
                qkv_ref.at[j, :, own_lanes], w_ref.at[:, pl.ds(j * 128, 128)], w_sem
            )
            for j in range(3)
        ]
        + [
            pltpu.make_async_copy(down_ref, w_ref.at[:, pl.ds(384, 128)], w_sem),
            pltpu.make_async_copy(beta_ref, w_ref.at[:, pl.ds(512, 128)], w_sem),
            pltpu.make_async_copy(out_ref.at[:, own_lanes], wo_ref, w_sem),
            pltpu.make_async_copy(all_up_ref.at[:, own_lanes], up_ref, w_sem),
        ]
    )
    sides = ((pieces[:2], pieces[2:8]), (pieces[8:10], pieces[10:16]))
    flights = [
        start_all(
            [
                copy
                for side in range(2)
                for copy in piece_copies(held_ref, *sides[side], side, array, at, sem)
            ]
        )
        for array, (held_ref, sem) in enumerate(((in_ref, in_sem), (grad_in_ref, grad_sem)))
    ]
    wait_all(weights)
    wait_all(flights[0])
    for block in range(4):
        rows = slice(block * 256, (block + 1) * 256)
        p_ref[rows, :] = dot2(in_ref[:, rows], w_ref[...], 0, 0)
    up = up_ref[...]
    bias = all_bias_ref[:, own_lanes]
    row, col = triangles()
    strict = (row > col)[None]
    lower = (row >= col)[None]
    eye = (row == col)[None]
    chunks = x_ref.shape[0]

    def prepare(group, carry):
        q, k, v, beta, gate, q_scale, k_scale = chunk_activations(p_ref, up, bias, group, count)
        e0, e1, e2, e3, final = decay_factors(-0.25 * gate)
        here = pl.ds(group * count, count)
        key_back = e2 * k
        coupling = jnp.where(strict, each(mA, e1 * k, key_back, 1, 1), 0.0)
        scores = jnp.where(lower, each(mA, e1 * q, key_back, 1, 1), 0.0)
        inverse = unit_lower_inverse(beta * coupling, mX)
        sv = each(mS, inverse, beta * v)
        sk = each(mS, inverse, beta * (e0 * k))
        key_end = e3 * k
        t_ref[here] = jnp.where(eye, final, 0.0) - each(mS, key_end, sk, 0, 0)
        off_ref[here] = each(mS, key_end, sv, 0, 0)
        qe_ref[here] = e0 * q - each(mS, scores, sk)
        lo_ref[here] = each(mS, scores, sv)
        x_ref[here] = inverse
        m_ref[here] = coupling
        s_ref[here] = scores
        sv_ref[here] = sv
        sk_ref[here] = sk
        return carry

    lax.fori_loop(0, chunks // count, prepare, 0)
    state = jnp.zeros((128, 128), f32)
    states_ref[0] = state
    for j in range(chunks - 1):
        state = mC(t_ref[j], state, 1, 0) + off_ref[j]
        states_ref[j + 1] = state
    for j in range(chunks):
        emitted = mS(qe_ref[j], states_ref[j], 1, 0) + lo_ref[j]
        mixed_ref[j * CHUNK : (j + 1) * CHUNK, :] = emitted.astype(bf16)
        tokens_ref[j, 512:640, :] = emitted.T.astype(bf16)


    wait_all(flights[1])
    for block in range(4):
        rows = slice(block * 256, (block + 1) * 256)
        do_ref[2 * block : 2 * block + 2] = dot2(grad_in_ref[:, rows], wo_ref[...], 0, 0).reshape(
            2, CHUNK, 128
        )
    for j in range(chunks):
        own_ref[j] = mB(qe_ref[j], do_ref[j], 0, 0)
    state = jnp.zeros((128, 128), f32)
    ds_ref[chunks - 1] = state
    for j in range(chunks - 1, 0, -1):
        state = mC(t_ref[j], state, 0, 0) + own_ref[j]
        ds_ref[j - 1] = state
    upper_ones = (row <= col).astype(bf16)
    extra_ref[...] = jnp.zeros_like(extra_ref)

    def finish(group, carry):
        q, k, v, beta, gate, q_scale, k_scale = chunk_activations(p_ref, up, bias, group, count)
        e0, e1, e2, e3, final = decay_factors(-0.25 * gate)
        here = pl.ds(group * count, count)
        d_out = do_ref[here]
        state = states_ref[here]
        d_state = ds_ref[here]
        scores = s_ref[here]
        coupling = m_ref[here]
        key_fwd = e1 * k
        key_back = e2 * k
        query_fwd = e1 * q
        key_start = e0 * k
        key_end = e3 * k
        solved = sv_ref[here] - each(mB, sk_ref[here], state)
        d_solved = each(mB, scores, d_out, 0, 0) + each(mB, key_end, d_state)
        weighted = each(mB, x_ref[here], d_solved, 0, 0)
        d_scores = jnp.where(lower, each(mB, d_out, solved, 1, 1), 0.0)
        d_strict = jnp.where(strict, -each(mB, weighted, solved, 1, 1), 0.0)
        remainder = v - each(mB, key_start, state)
        d_beta = jnp.sum(weighted * remainder, axis=-1, keepdims=True) + jnp.sum(
            d_strict * coupling, axis=-1, keepdims=True
        )
        d_coupling = beta * d_strict
        d_value = beta * weighted
        d_query_start = each(mB, d_out, state, 1, 1)
        d_key_start = -each(mB, d_value, state, 1, 1)
        d_key_end = each(mB, solved, d_state, 1, 1)
        d_key_fwd = each(mB, d_coupling, key_back)
        d_key_back = each(mB, d_coupling, key_fwd, 0, 0) + each(mB, d_scores, query_fwd, 0, 0)
        d_query_fwd = each(mB, d_scores, key_back)
        product = d_state * state
        d_final = jnp.sum(
            jnp.stack([product[i].T for i in range(count)]), axis=1, keepdims=True
        )
        d_query = e1 * d_query_fwd + e0 * d_query_start
        ahead = e1 * d_key_fwd + e0 * d_key_start
        behind = e2 * d_key_back
        ending = e3 * d_key_end
        d_key = ahead + behind + ending
        d_total = q * d_query + k * (ahead - behind - ending)
        last = jnp.sum(k * ending, axis=1, keepdims=True) + final * d_final
        d_log = ones_product(upper_ones, d_total) + last
        d_gate = d_log * (-0.25 * gate * (1.0 - gate))
        d_query = q_scale * (d_query - q * jnp.sum(q * d_query, axis=-1, keepdims=True))
        d_key = k_scale * (d_key - k * jnp.sum(k * d_key, axis=-1, keepdims=True))
        d_logit = d_beta * beta * (1.0 - beta)
        where = pl.ds(pl.multiple_of(group * (count * CHUNK), count * CHUNK), count * CHUNK)
        flat = lambda value: value.reshape(count * CHUNK, 128)
        gate_low = flat(d_gate).astype(bf16)
        for index, part in enumerate((d_query, d_key, d_value, d_gate)):
            lanes = slice(index * 128, (index + 1) * 128)
            if index < 3:
                right_ref[where, lanes] = flat(part).astype(bf16)
            else:
                right_ref[where, lanes] = dot2(gate_low, up, 1, 1).astype(bf16)
            for i in range(count):
                tokens_ref[group * count + i, lanes, :] = part[i].T.astype(bf16)
        for i in range(count):
            lanes = pl.ds(pl.multiple_of((group * count + i) * CHUNK, CHUNK), CHUNK)
            row_logit = d_logit[i].T[0:16].astype(bf16)
            logit_ref[:, lanes] = row_logit
            tokens_ref[group * count + i, 640:656, :] = row_logit
        extra_ref[0:128, :] += dot2(p_ref[where, 384:512].astype(bf16), gate_low, 0, 0)
        extra_ref[128:129, :] += jnp.sum(flat(d_gate), axis=0, keepdims=True)
        return carry

    lax.fori_loop(0, chunks // count, finish, 0)
    for x in range(4):
        features = slice(x * 576, (x + 1) * 576)
        piece = dot2(in_ref[features, :], right_ref[...], 1, 0)
        rows_ref[:, 0:384] = piece[:, 0:384]
        rows_ref[:, 384:512] = dot2(grad_in_ref[features, :], mixed_ref[...], 1, 0)
        rows_ref[:, 512:640] = piece[:, 384:512]
        for side, ref in enumerate((keep_ref, give_ref)):
            start = (core if side == 0 else 1 - core) * 288
            ref[x] = rows_ref[pl.ds(pl.multiple_of(start, 8), 288), 512:640].astype(bf16)
        for half in range(2):
            index = x * 2 + half
            beta = dot2(logit_ref[...], in_ref[index * 288 : (index + 1) * 288, :], 1, 1)
            first = 136 + index * 3
            extra_ref[first : first + 1, :] = beta[0:1, 0:128]
            extra_ref[first + 1 : first + 2, :] = beta[0:1, 128:256]
            extra_ref[first + 2 : first + 3, 0:32] = beta[0:1, 256:288]
            for owner in range(4):
                start = owner * 72 + half * 288
                tile_ref[owner, x, half] = rows_ref[start : start + 72, 0:512].astype(bf16)


TOKENS = 128


def output_kernel(
    at_ref, heads_ref, w_ref, wo_ref, down_ref, up_ref, beta_ref,
    out0_ref, out1_ref, out2_ref, out3_ref,
    right_ref, low_ref, logit_ref, term_ref,
):
    step = pl.program_id(0)
    block = out0_ref.shape[1]

    @pl.when(step == 0)
    def prepare():
        for h in range(8):
            rows = slice(h * 128, (h + 1) * 128)
            for index, part in enumerate((0, 1, 2, 4, 3)):
                right_ref[index, rows, :] = heads_ref[h, part * 128 : (part + 1) * 128, :]
            logit_ref[h : h + 1, :] = heads_ref[h, 640:656, :].astype(f32)[0:1]
        low_ref[...] = dot2(up_ref[...], right_ref[4], 1, 0).astype(bf16)
        term_ref[...] = dot2(beta_ref[...], logit_ref[...].astype(bf16), 0, 0)

    share = dot2(wo_ref[...], right_ref[3], 1, 0)
    first = lax.rem(at_ref[3] + step, 4) * block
    part = term_ref[pl.ds(pl.multiple_of(first, 8), block), :]
    part += dot2(w_ref[0], right_ref[0], 1, 0)
    part += dot2(w_ref[1], right_ref[1], 1, 0)
    part += dot2(w_ref[2], right_ref[2], 1, 0)
    part += dot2(down_ref[...], low_ref[...], 1, 0)
    for by, ref in enumerate((out0_ref, out1_ref, out2_ref, out3_ref)):

        @pl.when(step == by)
        def store(ref=ref):
            ref[0] = share.astype(bf16)
            ref[1] = part.astype(bf16)


def small_kernel(
    at_ref, low_ref, low2_ref, extra_ref, extra2_ref, down_ref, up_ref, bias_ref, beta_ref
):
    z, core, dp = at_ref[0], at_ref[1], at_ref[2]
    for side, (rows_ref, more_ref) in enumerate(((low_ref, extra_ref), (low2_ref, extra2_ref))):
        half = core if side == 0 else 1 - core
        for i in range(4):
            low = rows_ref[i].astype(f32)
            place = lax.rem(dp + (4 - i), 4)
            for zp in range(4):
                down_ref[zp, half, place] = low[zp * 72 : (zp + 1) * 72]
            extra = more_ref[i].astype(f32)
            head = lax.rem(z + (4 - i), 4) * 2 + half
            up_ref[:, pl.ds(pl.multiple_of(head * 128, 128), 128)] = extra[0:128]
            bias_ref[pl.ds(head, 1), :] = extra[128:129]
            beta_ref[head] = extra[136:160]


def place_kernel(in_ref, qkv_ref, out_ref):
    for h in range(8):
        lanes = slice(h * 128, (h + 1) * 128)
        for j in range(3):
            qkv_ref[j, :, lanes] = in_ref[h, :, j * 128 : (j + 1) * 128]
        out_ref[:, lanes] = in_ref[h, :, 384:512]


def vmem(n):
    return [pl.BlockSpec(memory_space=pltpu.VMEM)] * n


def anywhere(n):
    return [pl.BlockSpec(memory_space=pl.ANY)] * n


def cost(flops, bytes_accessed):
    return pl.CostEstimate(flops=flops, bytes_accessed=bytes_accessed, transcendentals=0)


def run_recurrence(at, pieces, qkv, out, down, beta, up, bias):
    chunks, tokens = 8, 1024
    shape = jax.ShapeDtypeStruct
    return pl.pallas_call(
        functools.partial(recurrence_kernel, three_pass, 4),
        out_shape=(shape((4, 4, 2, 72, 512), bf16), shape((chunks, 656, 128), bf16))
        + (shape((4, 288, 128), bf16),) * 2
        + (shape((160, 128), f32),),
        in_specs=[pl.BlockSpec(memory_space=pltpu.SMEM)] + anywhere(len(pieces) + 5) + vmem(1),
        out_specs=tuple(vmem(5)),
        scratch_shapes=[pltpu.VMEM((tokens, 128), bf16)]
        + [pltpu.VMEM((2304, tokens), bf16)] * 2
        + [pltpu.VMEM((tokens, 640), f32)]
        + [pltpu.VMEM((chunks, 128, 128), f32)] * 12
        + [
            pltpu.VMEM((tokens, 512), bf16),
            pltpu.VMEM((576, 640), f32),
            pltpu.VMEM((16, tokens), bf16),
            pltpu.VMEM((2304, 640), bf16),
            pltpu.VMEM((2304, 128), bf16),
            pltpu.VMEM((128, 128), bf16),
            pltpu.SemaphoreType.DMA,
            pltpu.SemaphoreType.DMA,
            pltpu.SemaphoreType.DMA,
        ],
        compiler_params=pltpu.CompilerParams(vmem_limit_bytes=52 << 20),
        cost_estimate=cost(16_000_000_000, 40_000_000),
        name="recurrence",
    )(at, *pieces, qkv, out, down, beta, up, bias)


def run_output(at, heads, w, wo, down, up, beta):
    block = w.shape[1] // 4

    def rows(step, at_ref):
        return (lax.rem(at_ref[3] + step, 4), 0)

    def deep_rows(step, at_ref):
        return (0, lax.rem(at_ref[3] + step, 4), 0)

    whole = lambda value: pl.BlockSpec(value.shape, lambda step, at_ref: (0,) * len(value.shape))
    out = jax.ShapeDtypeStruct((2, block, TOKENS), bf16)
    return pl.pallas_call(
        output_kernel,
        out_shape=(out,) * 4,
        grid_spec=pltpu.PrefetchScalarGridSpec(
            num_scalar_prefetch=1,
            grid=(4,),
            in_specs=[
                whole(heads),
                pl.BlockSpec((3, block, w.shape[2]), deep_rows),
                pl.BlockSpec((block, wo.shape[1]), rows),
                pl.BlockSpec((block, down.shape[1]), rows),
                whole(up),
                whole(beta),
            ],
            out_specs=tuple([whole(out)] * 4),
            scratch_shapes=[
                pltpu.VMEM((5, 1024, TOKENS), bf16),
                pltpu.VMEM((128, TOKENS), bf16),
                pltpu.VMEM((8, TOKENS), f32),
                pltpu.VMEM((w.shape[1], TOKENS), f32),
            ],
        ),
        compiler_params=pltpu.CompilerParams(vmem_limit_bytes=48 << 20),
        cost_estimate=cost(3_000_000_000, 200_000_000),
        name="output",
    )(at, heads, w, wo, down, up, beta)


def run_small(at, *parts):
    shape = jax.ShapeDtypeStruct
    return pl.pallas_call(
        small_kernel,
        out_shape=(
            shape((4, 2, 4, 72, 128), f32),
            shape((128, 1024), f32),
            shape((8, 128), f32),
            shape((8, 24, 128), f32),
        ),
        in_specs=[pl.BlockSpec(memory_space=pltpu.SMEM)] + vmem(4),
        out_specs=tuple(vmem(4)),
        cost_estimate=cost(1_000_000, 4_000_000),
        name="small",
    )(at, *parts)


def run_place(moved):
    rows = moved.shape[1]
    return pl.pallas_call(
        place_kernel,
        out_shape=(
            jax.ShapeDtypeStruct((3, rows, 1024), bf16),
            jax.ShapeDtypeStruct((rows, 1024), bf16),
        ),
        in_specs=vmem(1),
        out_specs=tuple(vmem(2)),
        cost_estimate=cost(1_000_000, 400_000_000),
        name="place",
    )(moved)


def turn(value, axis, by):
    count = lax.axis_size(axis)
    return lax.ppermute(value, axis, [(i, (i + by) % count) for i in range(count)])


def swap(value):
    return lax.ppermute(value, "core", [(0, 1), (1, 0)])


def selector(value, count):
    return lax.broadcasted_iota(jnp.int32, (count,) + (1,) * value.ndim, 0)


def ordered(own, other, position):
    return jnp.where(selector(own, 2) == position, own[None], other[None])


def stacked(members):
    at = selector(members[0], 4)
    low = jnp.where(at == 0, members[0][None], members[1][None])
    high = jnp.where(at == 2, members[2][None], members[3][None])
    return jnp.where(at < 2, low, high)


def ring_sum(own, arrived):
    wide = [member.astype(f32) for member in [own] + arrived]
    return (wide[0] + wide[2]) + (wide[1] + wide[3])


def scatter_sum(pick, axis):
    index = lax.axis_index(axis)
    arrived = [turn(pick((index + by) % 4), axis, by) for by in (1, 2, 3)]
    return ring_sum(pick(index), arrived)


def shards(
    inputs, output_grad, qkv_weight, out_weight, down_weight, up_weight, beta_weight, gate_bias
):
    z, core, dp, head = (lax.axis_index(name) for name in ("z", "core", "dp", "head"))
    at = jnp.stack([z, core, dp, head]).astype(jnp.int32)
    width = qkv_weight.shape[0]
    piece = width // 8
    spot = z * 2 + core
    steps = (1, 2, 3)

    both = jnp.stack([inputs[0].T, output_grad[0].T])
    own = lax.dynamic_slice_in_dim(both, core * piece, piece, axis=1)
    got = swap(lax.dynamic_slice_in_dim(both, (1 - core) * piece, piece, axis=1))

    early = [
        stacked([own] + [turn(own, "z", by) for by in steps]),
        stacked([got] + [turn(got, "head", by) for by in steps]),
    ]
    late = [turn(early[0], "head", by) for by in steps]
    late += [turn(early[1], "z", by) for by in steps]
    pieces = early + late
    pieces += [swap(member) for member in pieces]

    beta_column = lax.dynamic_slice_in_dim(beta_weight, spot, 1, axis=1)
    qkv_parts = jnp.swapaxes(qkv_weight, 0, 1)
    outs = run_recurrence(
        at, pieces, qkv_parts, out_weight, down_weight,
        jnp.broadcast_to(beta_column, (width, 128)), up_weight, gate_bias[None],
    )
    tile, tokens, down_keep, down_give, extra = outs

    summed = lax.psum_scatter(tile, "dp", scatter_dimension=0, tiled=False)
    heads = lax.all_to_all(tokens, ("z", "core"), 0, 0, tiled=True)
    down_got = swap(down_give)

    down_tile = (down_keep.astype(f32) + down_got.astype(f32)).astype(bf16)
    down_tile = down_tile.reshape(4, 4, piece // 4, 128)
    extra = extra.astype(bf16)

    def first_pick(index):
        rows = lax.dynamic_index_in_dim(down_tile, index, axis=1, keepdims=False)
        return jnp.concatenate([rows.reshape(piece, 128), extra], axis=0)

    first = scatter_sum(first_pick, "dp").astype(bf16)
    low_rows = first[:piece]
    low_rows = ring_sum(low_rows, [turn(low_rows, "head", by) for by in steps]).astype(bf16)
    shares = run_output(
        at, heads, qkv_parts, out_weight, down_weight, up_weight,
        beta_weight.T,
    )
    low_rows, shares = lax.optimization_barrier((low_rows, shares))
    load = jnp.concatenate([low_rows, first[piece:]], axis=0)
    came = [turn(load, "z", by) for by in steps]
    low_rows = ring_sum(load[:piece], [member[:piece] for member in came]).astype(bf16)
    extras = stacked([member[piece:] for member in [load] + came])
    extras_swapped = swap(extras)
    low_all = stacked([low_rows] + [turn(low_rows, "dp", by) for by in steps])
    down_grad, up_grad, bias_grad, beta_grad = run_small(
        at, low_all, swap(low_all), extras, extras_swapped
    )
    down_grad = down_grad.reshape(width, 128)
    bias_grad = bias_grad.reshape(1024)
    beta_grad = beta_grad.reshape(8, 8, 384)[:, :, :piece].reshape(8, width).T

    results = ring_sum(shares[0], [turn(shares[by], "head", by) for by in steps]).astype(bf16)
    layer_out = results[0].T[None]
    input_grad = results[1].T[None]

    moved = lax.all_to_all(
        summed.reshape(8, piece // 4, 512), ("z", "core"), 0, 0, tiled=True
    )
    qkv_grad, out_grad = run_place(moved)
    qkv_grad = jnp.swapaxes(qkv_grad, 0, 1)
    return (layer_out, input_grad, qkv_grad, out_grad, up_grad, down_grad, beta_grad, bias_grad)


def solution(mesh):
    fine = Mesh(
        mesh.devices.reshape(4, 2, mesh.shape["dp"], mesh.shape["head"]),
        ("z", "core", "dp", "head"),
    )
    context = ("z", "core")
    return jax.shard_map(
        shards,
        mesh=fine,
        in_specs=(
            P("dp", context, "head"),
            P("dp", context, "head"),
            P(None, None, "head"),
            P(None, "head"),
            P(),
            P(None, "head"),
            P(None, "head"),
            P("head"),
        ),
        out_specs=(
            P("dp", context, "head"),
            P("dp", context, "head"),
            P(context + ("dp",), None, "head"),
            P(context + ("dp",), "head"),
            P(None, "head"),
            P(),
            P(None, "head"),
            P("head"),
        ),
        check_vma=False,
    )
```

```python
import functools
import jax
import jax.numpy as jnp
from jax import lax
from jax.experimental import pallas as pl
from jax.experimental.pallas import tpu as pltpu
from jax.sharding import Mesh
from jax.sharding import PartitionSpec as P

bf16 = jnp.bfloat16
f32 = jnp.float32
CHUNK = 128
epsilon = 1e-06


def dot2(left, right, ca, cb):
    return lax.dot_general(left, right, (((ca,), (cb,)), ((), ())), preferred_element_type=f32)


def halves(value):
    high = value.astype(bf16)
    return high, (value - high.astype(f32)).astype(bf16)


def one_pass(left, right, ca, cb):
    return dot2(left.astype(bf16), right.astype(bf16), ca, cb)


def three_pass(left, right, ca, cb):
    lh, ll = halves(left)
    rh, rl = halves(right)
    return dot2(lh, rh, ca, cb) + (dot2(lh, rl, ca, cb) + dot2(ll, rh, ca, cb))


def each(func, left, right, ca=1, cb=0):
    return jnp.stack([func(left[i], right[i], ca, cb) for i in range(left.shape[0])])


def ones_product(ones, value):
    high, low = halves(value)
    return jnp.stack(
        [dot2(ones, high[i], 1, 0) + dot2(ones, low[i], 1, 0) for i in range(value.shape[0])]
    )


def triangles():
    row = lax.broadcasted_iota(jnp.int32, (CHUNK, CHUNK), 0)
    col = lax.broadcasted_iota(jnp.int32, (CHUNK, CHUNK), 1)
    return row, col


def unit_lower_inverse(strict_part, mul):
    row, col = triangles()
    eye = (row == col).astype(f32)
    joined = (row >> 1) == (col >> 1)
    inverse = eye[None] - jnp.where(joined[None], strict_part, 0.0)
    level = 1
    while (1 << level) < CHUNK:
        across = ((row >> (level + 1)) == (col >> (level + 1))) & ((row >> level) != (col >> level))
        below = jnp.where(across[None], strict_part, 0.0)
        inverse = inverse - each(mul, inverse, each(mul, below, inverse))
        level += 1
    return inverse


def decay_factors(logs):
    row, col = triangles()
    lower = (row >= col).astype(bf16)
    total = ones_product(lower, logs)
    middle = total[:, CHUNK // 2 - 1 : CHUNK // 2, :]
    final = total[:, CHUNK - 1 :, :]
    return (
        jnp.exp(total),
        jnp.exp(total - middle),
        jnp.exp(middle - total),
        jnp.exp(final - total),
        jnp.exp(final),
    )


def normalized(values):
    scale = lax.rsqrt(jnp.sum(values * values, axis=-1, keepdims=True) + epsilon)
    return values * scale, scale


def sigmoid(value):
    return 1.0 / (1.0 + jnp.exp(-value))


def chunk_activations(p_ref, up, bias, group, count):
    rows = pl.ds(pl.multiple_of(group * (count * CHUNK), count * CHUNK), count * CHUNK)

    def part(index):
        return p_ref[rows, index * 128 : (index + 1) * 128]

    def blocked(value):
        return value.reshape(count, CHUNK, value.shape[-1])

    queries, q_scale = normalized(part(0))
    key_rows, k_scale = normalized(part(1))
    gate = sigmoid(dot2(part(3).astype(bf16), up, 1, 0) + bias)
    beta = sigmoid(part(4))
    return (
        blocked(queries),
        blocked(key_rows),
        blocked(part(2)),
        blocked(beta),
        blocked(gate),
        blocked(q_scale),
        blocked(k_scale),
    )


def start_all(copies):
    for copy in copies:
        copy.start()
    return copies


def wait_all(copies):
    for copy in copies:
        copy.wait()


def piece_copies(out_ref, early_refs, late_refs, side, array, at, sem):
    z, core, head = at[0], at[1], at[3]
    groups = [[], [], [], []]
    for own_tokens in (True, False):
        token_core = core if own_tokens == (side == 0) else 1 - core
        for first in range(4):
            for second in range(4):
                dx, dz = (first, second) if own_tokens else (second, first)
                if first == 0:
                    piece = early_refs[0 if own_tokens else 1].at[second, array]
                else:
                    piece = late_refs[first - 1 + (0 if own_tokens else 3)].at[second, array]
                block = lax.rem(z + (4 - dz), 4) * 2 + token_core
                lanes = pl.ds(pl.multiple_of(block * 128, 128), 128)
                half = core if side == 0 else 1 - core
                first_row = (lax.rem(head + (4 - dx), 4) * 2 + half) * 288
                place = out_ref.at[pl.ds(pl.multiple_of(first_row, 16), 288), lanes]
                groups[dz].append(pltpu.make_async_copy(piece, place, sem.at[dz]))
    return groups


def recurrence_kernel(
    mul, count, at_ref, *refs,
):
    pieces, refs = refs[:16], refs[16:]
    (
        qkv_ref, out_ref, down_ref, beta_ref, all_up_ref, all_bias_ref,
        tile_ref, tokens_ref, keep_ref, give_ref, extra_ref,
        mixed_ref, in_ref, grad_in_ref, p_ref, x_ref, m_ref, s_ref, t_ref, qe_ref, sv_ref, sk_ref,
        states_ref, off_ref, do_ref, own_ref, ds_ref, right_ref, rows_ref, logit_ref,
        w_ref, wo_ref, up_ref, in_sem, grad_sem, w_sem,
    ) = refs
    mA = mX = mS = mC = mB = mul
    lo_ref = own_ref
    at = [at_ref[i] for i in range(4)]
    core = at[1]
    own_lanes = pl.ds(pl.multiple_of((at[0] * 2 + core) * 128, 128), 128)
    weights = start_all(
        [
            pltpu.make_async_copy(
                qkv_ref.at[j, :, own_lanes], w_ref.at[:, pl.ds(j * 128, 128)], w_sem
            )
            for j in range(3)
        ]
        + [
            pltpu.make_async_copy(down_ref, w_ref.at[:, pl.ds(384, 128)], w_sem),
            pltpu.make_async_copy(beta_ref, w_ref.at[:, pl.ds(512, 128)], w_sem),
            pltpu.make_async_copy(out_ref.at[:, own_lanes], wo_ref, w_sem),
            pltpu.make_async_copy(all_up_ref.at[:, own_lanes], up_ref, w_sem),
        ]
    )
    sides = ((pieces[:2], pieces[2:8]), (pieces[8:10], pieces[10:16]))
    flights = []
    for array, (held_ref, sem) in enumerate(((in_ref, in_sem), (grad_in_ref, grad_sem))):
        halves_of = [
            piece_copies(held_ref, *sides[side], side, array, at, sem) for side in range(2)
        ]
        flights.append([start_all(halves_of[0][dz] + halves_of[1][dz]) for dz in range(4)])
    wait_all(weights)
    token_rows = [
        pl.ds(pl.multiple_of(lax.rem(at[0] + (4 - dz), 4) * 256, 256), 256) for dz in range(4)
    ]
    for dz, rows in enumerate(token_rows):
        wait_all(flights[0][dz])
        p_ref[rows, :] = dot2(in_ref[:, rows], w_ref[...], 0, 0)
    up = up_ref[...]
    bias = all_bias_ref[:, own_lanes]
    row, col = triangles()
    strict = (row > col)[None]
    lower = (row >= col)[None]
    eye = (row == col)[None]
    chunks = x_ref.shape[0]

    def prepare(group, carry):
        q, k, v, beta, gate, q_scale, k_scale = chunk_activations(p_ref, up, bias, group, count)
        e0, e1, e2, e3, final = decay_factors(-0.25 * gate)
        here = pl.ds(group * count, count)
        key_back = e2 * k
        coupling = jnp.where(strict, each(mA, e1 * k, key_back, 1, 1), 0.0)
        scores = jnp.where(lower, each(mA, e1 * q, key_back, 1, 1), 0.0)
        inverse = unit_lower_inverse(beta * coupling, mX)
        sv = each(mS, inverse, beta * v)
        sk = each(mS, inverse, beta * (e0 * k))
        key_end = e3 * k
        t_ref[here] = jnp.where(eye, final, 0.0) - each(mS, key_end, sk, 0, 0)
        off_ref[here] = each(mS, key_end, sv, 0, 0)
        qe_ref[here] = e0 * q - each(mS, scores, sk)
        lo_ref[here] = each(mS, scores, sv)
        x_ref[here] = inverse
        m_ref[here] = coupling
        s_ref[here] = scores
        sv_ref[here] = sv
        sk_ref[here] = sk
        return carry

    lax.fori_loop(0, chunks // count, prepare, 0)
    state = jnp.zeros((128, 128), f32)
    states_ref[0] = state
    for j in range(chunks - 1):
        state = mC(t_ref[j], state, 1, 0) + off_ref[j]
        states_ref[j + 1] = state
    for j in range(chunks):
        emitted = mS(qe_ref[j], states_ref[j], 1, 0) + lo_ref[j]
        mixed_ref[j * CHUNK : (j + 1) * CHUNK, :] = emitted.astype(bf16)
        tokens_ref[j, 512:640, :] = emitted.T.astype(bf16)


    for group in flights[1]:
        wait_all(group)
    for block in range(4):
        rows = slice(block * 256, (block + 1) * 256)
        do_ref[2 * block : 2 * block + 2] = dot2(grad_in_ref[:, rows], wo_ref[...], 0, 0).reshape(
            2, CHUNK, 128
        )
    for j in range(chunks):
        own_ref[j] = mB(qe_ref[j], do_ref[j], 0, 0)
    state = jnp.zeros((128, 128), f32)
    ds_ref[chunks - 1] = state
    for j in range(chunks - 1, 0, -1):
        state = mC(t_ref[j], state, 0, 0) + own_ref[j]
        ds_ref[j - 1] = state
    upper_ones = (row <= col).astype(bf16)
    extra_ref[...] = jnp.zeros_like(extra_ref)

    def finish(group, carry):
        q, k, v, beta, gate, q_scale, k_scale = chunk_activations(p_ref, up, bias, group, count)
        e0, e1, e2, e3, final = decay_factors(-0.25 * gate)
        here = pl.ds(group * count, count)
        d_out = do_ref[here]
        state = states_ref[here]
        d_state = ds_ref[here]
        scores = s_ref[here]
        coupling = m_ref[here]
        key_fwd = e1 * k
        key_back = e2 * k
        query_fwd = e1 * q
        key_start = e0 * k
        key_end = e3 * k
        solved = sv_ref[here] - each(mB, sk_ref[here], state)
        d_solved = each(mB, scores, d_out, 0, 0) + each(mB, key_end, d_state)
        weighted = each(mB, x_ref[here], d_solved, 0, 0)
        d_scores = jnp.where(lower, each(mB, d_out, solved, 1, 1), 0.0)
        d_strict = jnp.where(strict, -each(mB, weighted, solved, 1, 1), 0.0)
        remainder = v - each(mB, key_start, state)
        d_beta = jnp.sum(weighted * remainder, axis=-1, keepdims=True) + jnp.sum(
            d_strict * coupling, axis=-1, keepdims=True
        )
        d_coupling = beta * d_strict
        d_value = beta * weighted
        d_query_start = each(mB, d_out, state, 1, 1)
        d_key_start = -each(mB, d_value, state, 1, 1)
        d_key_end = each(mB, solved, d_state, 1, 1)
        d_key_fwd = each(mB, d_coupling, key_back)
        d_key_back = each(mB, d_coupling, key_fwd, 0, 0) + each(mB, d_scores, query_fwd, 0, 0)
        d_query_fwd = each(mB, d_scores, key_back)
        product = d_state * state
        d_final = jnp.sum(
            jnp.stack([product[i].T for i in range(count)]), axis=1, keepdims=True
        )
        d_query = e1 * d_query_fwd + e0 * d_query_start
        ahead = e1 * d_key_fwd + e0 * d_key_start
        behind = e2 * d_key_back
        ending = e3 * d_key_end
        d_key = ahead + behind + ending
        d_total = q * d_query + k * (ahead - behind - ending)
        last = jnp.sum(k * ending, axis=1, keepdims=True) + final * d_final
        d_log = ones_product(upper_ones, d_total) + last
        d_gate = d_log * (-0.25 * gate * (1.0 - gate))
        d_query = q_scale * (d_query - q * jnp.sum(q * d_query, axis=-1, keepdims=True))
        d_key = k_scale * (d_key - k * jnp.sum(k * d_key, axis=-1, keepdims=True))
        d_logit = d_beta * beta * (1.0 - beta)
        where = pl.ds(pl.multiple_of(group * (count * CHUNK), count * CHUNK), count * CHUNK)
        flat = lambda value: value.reshape(count * CHUNK, 128)
        gate_low = flat(d_gate).astype(bf16)
        for index, part in enumerate((d_query, d_key, d_value, d_gate)):
            lanes = slice(index * 128, (index + 1) * 128)
            if index < 3:
                right_ref[where, lanes] = flat(part).astype(bf16)
            else:
                right_ref[where, lanes] = dot2(gate_low, up, 1, 1).astype(bf16)
            for i in range(count):
                tokens_ref[group * count + i, lanes, :] = part[i].T.astype(bf16)
        for i in range(count):
            lanes = pl.ds(pl.multiple_of((group * count + i) * CHUNK, CHUNK), CHUNK)
            row_logit = d_logit[i].T[0:16].astype(bf16)
            logit_ref[:, lanes] = row_logit
            tokens_ref[group * count + i, 640:656, :] = row_logit
        extra_ref[0:128, :] += dot2(p_ref[where, 384:512].astype(bf16), gate_low, 0, 0)
        extra_ref[128:129, :] += jnp.sum(flat(d_gate), axis=0, keepdims=True)
        return carry

    lax.fori_loop(0, chunks // count, finish, 0)
    for x in range(4):
        features = slice(x * 576, (x + 1) * 576)
        piece = dot2(in_ref[features, :], right_ref[...], 1, 0)
        rows_ref[:, 0:384] = piece[:, 0:384]
        rows_ref[:, 384:512] = dot2(grad_in_ref[features, :], mixed_ref[...], 1, 0)
        rows_ref[:, 512:640] = piece[:, 384:512]
        for side, ref in enumerate((keep_ref, give_ref)):
            start = (core if side == 0 else 1 - core) * 288
            ref[x] = rows_ref[pl.ds(pl.multiple_of(start, 8), 288), 512:640].astype(bf16)
        for half in range(2):
            index = x * 2 + half
            beta = dot2(logit_ref[...], in_ref[index * 288 : (index + 1) * 288, :], 1, 1)
            first = 136 + index * 3
            extra_ref[first : first + 1, :] = beta[0:1, 0:128]
            extra_ref[first + 1 : first + 2, :] = beta[0:1, 128:256]
            extra_ref[first + 2 : first + 3, 0:32] = beta[0:1, 256:288]
            for owner in range(4):
                start = owner * 72 + half * 288
                tile_ref[owner, x, half] = rows_ref[start : start + 72, 0:512].astype(bf16)


TOKENS = 128


def output_kernel(
    at_ref, heads_ref, w_ref, wo_ref, down_ref, up_ref, beta_ref,
    out0_ref, out1_ref, out2_ref, out3_ref,
    right_ref, low_ref, logit_ref, term_ref,
):
    step = pl.program_id(0)
    block = out0_ref.shape[1]

    @pl.when(step == 0)
    def prepare():
        for h in range(8):
            rows = slice(h * 128, (h + 1) * 128)
            for index, part in enumerate((0, 1, 2, 4, 3)):
                right_ref[index, rows, :] = heads_ref[h, part * 128 : (part + 1) * 128, :]
            logit_ref[h : h + 1, :] = heads_ref[h, 640:656, :].astype(f32)[0:1]
        low_ref[...] = dot2(up_ref[...], right_ref[4], 1, 0).astype(bf16)
        term_ref[...] = dot2(beta_ref[...], logit_ref[...].astype(bf16), 0, 0)

    share = dot2(wo_ref[...], right_ref[3], 1, 0)
    first = lax.rem(at_ref[3] + step, 4) * block
    part = term_ref[pl.ds(pl.multiple_of(first, 8), block), :]
    part += dot2(w_ref[0], right_ref[0], 1, 0)
    part += dot2(w_ref[1], right_ref[1], 1, 0)
    part += dot2(w_ref[2], right_ref[2], 1, 0)
    part += dot2(down_ref[...], low_ref[...], 1, 0)
    for by, ref in enumerate((out0_ref, out1_ref, out2_ref, out3_ref)):

        @pl.when(step == by)
        def store(ref=ref):
            ref[0] = share.astype(bf16)
            ref[1] = part.astype(bf16)


def small_kernel(
    at_ref, low_ref, low2_ref, extra_ref, extra2_ref, down_ref, up_ref, bias_ref, beta_ref
):
    z, core, dp = at_ref[0], at_ref[1], at_ref[2]
    for side, (rows_ref, more_ref) in enumerate(((low_ref, extra_ref), (low2_ref, extra2_ref))):
        half = core if side == 0 else 1 - core
        for i in range(4):
            low = rows_ref[i].astype(f32)
            place = lax.rem(dp + (4 - i), 4)
            for zp in range(4):
                down_ref[zp, half, place] = low[zp * 72 : (zp + 1) * 72]
            extra = more_ref[i].astype(f32)
            head = lax.rem(z + (4 - i), 4) * 2 + half
            up_ref[:, pl.ds(pl.multiple_of(head * 128, 128), 128)] = extra[0:128]
            bias_ref[pl.ds(head, 1), :] = extra[128:129]
            beta_ref[head] = extra[136:160]


def place_kernel(in_ref, qkv_ref, out_ref):
    for h in range(8):
        lanes = slice(h * 128, (h + 1) * 128)
        for j in range(3):
            qkv_ref[j, :, lanes] = in_ref[h, :, j * 128 : (j + 1) * 128]
        out_ref[:, lanes] = in_ref[h, :, 384:512]


def vmem(n):
    return [pl.BlockSpec(memory_space=pltpu.VMEM)] * n


def anywhere(n):
    return [pl.BlockSpec(memory_space=pl.ANY)] * n


def cost(flops, bytes_accessed):
    return pl.CostEstimate(flops=flops, bytes_accessed=bytes_accessed, transcendentals=0)


def run_recurrence(at, pieces, qkv, out, down, beta, up, bias):
    chunks, tokens = 8, 1024
    shape = jax.ShapeDtypeStruct
    return pl.pallas_call(
        functools.partial(recurrence_kernel, three_pass, 4),
        out_shape=(shape((4, 4, 2, 72, 512), bf16), shape((chunks, 656, 128), bf16))
        + (shape((4, 288, 128), bf16),) * 2
        + (shape((160, 128), f32),),
        in_specs=[pl.BlockSpec(memory_space=pltpu.SMEM)] + anywhere(len(pieces) + 5) + vmem(1),
        out_specs=tuple(vmem(5)),
        scratch_shapes=[pltpu.VMEM((tokens, 128), bf16)]
        + [pltpu.VMEM((2304, tokens), bf16)] * 2
        + [pltpu.VMEM((tokens, 640), f32)]
        + [pltpu.VMEM((chunks, 128, 128), f32)] * 12
        + [
            pltpu.VMEM((tokens, 512), bf16),
            pltpu.VMEM((576, 640), f32),
            pltpu.VMEM((16, tokens), bf16),
            pltpu.VMEM((2304, 640), bf16),
            pltpu.VMEM((2304, 128), bf16),
            pltpu.VMEM((128, 128), bf16),
            pltpu.SemaphoreType.DMA((4,)),
            pltpu.SemaphoreType.DMA((4,)),
            pltpu.SemaphoreType.DMA,
        ],
        compiler_params=pltpu.CompilerParams(vmem_limit_bytes=52 << 20),
        cost_estimate=cost(16_000_000_000, 40_000_000),
        name="recurrence",
    )(at, *pieces, qkv, out, down, beta, up, bias)


def run_output(at, heads, w, wo, down, up, beta):
    block = w.shape[1] // 4

    def rows(step, at_ref):
        return (lax.rem(at_ref[3] + step, 4), 0)

    def deep_rows(step, at_ref):
        return (0, lax.rem(at_ref[3] + step, 4), 0)

    whole = lambda value: pl.BlockSpec(value.shape, lambda step, at_ref: (0,) * len(value.shape))
    out = jax.ShapeDtypeStruct((2, block, TOKENS), bf16)
    return pl.pallas_call(
        output_kernel,
        out_shape=(out,) * 4,
        grid_spec=pltpu.PrefetchScalarGridSpec(
            num_scalar_prefetch=1,
            grid=(4,),
            in_specs=[
                whole(heads),
                pl.BlockSpec((3, block, w.shape[2]), deep_rows),
                pl.BlockSpec((block, wo.shape[1]), rows),
                pl.BlockSpec((block, down.shape[1]), rows),
                whole(up),
                whole(beta),
            ],
            out_specs=tuple([whole(out)] * 4),
            scratch_shapes=[
                pltpu.VMEM((5, 1024, TOKENS), bf16),
                pltpu.VMEM((128, TOKENS), bf16),
                pltpu.VMEM((8, TOKENS), f32),
                pltpu.VMEM((w.shape[1], TOKENS), f32),
            ],
        ),
        compiler_params=pltpu.CompilerParams(vmem_limit_bytes=48 << 20),
        cost_estimate=cost(3_000_000_000, 200_000_000),
        name="output",
    )(at, heads, w, wo, down, up, beta)


def run_small(at, *parts):
    shape = jax.ShapeDtypeStruct
    return pl.pallas_call(
        small_kernel,
        out_shape=(
            shape((4, 2, 4, 72, 128), f32),
            shape((128, 1024), f32),
            shape((8, 128), f32),
            shape((8, 24, 128), f32),
        ),
        in_specs=[pl.BlockSpec(memory_space=pltpu.SMEM)] + vmem(4),
        out_specs=tuple(vmem(4)),
        cost_estimate=cost(1_000_000, 4_000_000),
        name="small",
    )(at, *parts)


def run_place(moved):
    rows = moved.shape[1]
    return pl.pallas_call(
        place_kernel,
        out_shape=(
            jax.ShapeDtypeStruct((3, rows, 1024), bf16),
            jax.ShapeDtypeStruct((rows, 1024), bf16),
        ),
        in_specs=vmem(1),
        out_specs=tuple(vmem(2)),
        cost_estimate=cost(1_000_000, 400_000_000),
        name="place",
    )(moved)


def turn(value, axis, by):
    count = lax.axis_size(axis)
    return lax.ppermute(value, axis, [(i, (i + by) % count) for i in range(count)])


def swap(value):
    return lax.ppermute(value, "core", [(0, 1), (1, 0)])


def selector(value, count):
    return lax.broadcasted_iota(jnp.int32, (count,) + (1,) * value.ndim, 0)


def ordered(own, other, position):
    return jnp.where(selector(own, 2) == position, own[None], other[None])


def stacked(members):
    at = selector(members[0], 4)
    low = jnp.where(at == 0, members[0][None], members[1][None])
    high = jnp.where(at == 2, members[2][None], members[3][None])
    return jnp.where(at < 2, low, high)


def ring_sum(own, arrived):
    wide = [member.astype(f32) for member in [own] + arrived]
    return (wide[0] + wide[2]) + (wide[1] + wide[3])


def scatter_sum(pick, axis):
    index = lax.axis_index(axis)
    arrived = [turn(pick((index + by) % 4), axis, by) for by in (1, 2, 3)]
    return ring_sum(pick(index), arrived)


def shards(
    inputs, output_grad, qkv_weight, out_weight, down_weight, up_weight, beta_weight, gate_bias
):
    z, core, dp, head = (lax.axis_index(name) for name in ("z", "core", "dp", "head"))
    at = jnp.stack([z, core, dp, head]).astype(jnp.int32)
    width = qkv_weight.shape[0]
    piece = width // 8
    spot = z * 2 + core
    steps = (1, 2, 3)

    both = jnp.stack([inputs[0].T, output_grad[0].T])
    own = lax.dynamic_slice_in_dim(both, core * piece, piece, axis=1)
    got = swap(lax.dynamic_slice_in_dim(both, (1 - core) * piece, piece, axis=1))

    early = [
        stacked([own] + [turn(own, "z", by) for by in steps]),
        stacked([got] + [turn(got, "head", by) for by in steps]),
    ]
    late = [turn(early[0], "head", by) for by in steps]
    late += [turn(early[1], "z", by) for by in steps]
    beta_column = lax.dynamic_slice_in_dim(beta_weight, spot, 1, axis=1)
    beta_wide = jnp.broadcast_to(beta_column, (width, 128))
    late[5], beta_wide = lax.optimization_barrier((late[5], beta_wide))
    pieces = early + late
    pieces += [swap(member) for member in pieces]

    qkv_parts = jnp.swapaxes(qkv_weight, 0, 1)
    outs = run_recurrence(
        at, pieces, qkv_parts, out_weight, down_weight,
        beta_wide, up_weight, gate_bias[None],
    )
    tile, tokens, down_keep, down_give, extra = outs

    summed = lax.psum_scatter(tile, "dp", scatter_dimension=0, tiled=False)
    heads = lax.all_to_all(tokens, ("z", "core"), 0, 0, tiled=True)
    down_got = swap(down_give)

    down_tile = (down_keep.astype(f32) + down_got.astype(f32)).astype(bf16)
    down_tile = down_tile.reshape(4, 4, piece // 4, 128)
    extra = extra.astype(bf16)

    def first_pick(index):
        rows = lax.dynamic_index_in_dim(down_tile, index, axis=1, keepdims=False)
        return jnp.concatenate([rows.reshape(piece, 128), extra], axis=0)

    first = scatter_sum(first_pick, "dp").astype(bf16)
    low_rows = first[:piece]
    low_rows = ring_sum(low_rows, [turn(low_rows, "head", by) for by in steps]).astype(bf16)
    shares = run_output(
        at, heads, qkv_parts, out_weight, down_weight, up_weight,
        beta_weight.T,
    )
    low_rows, shares = lax.optimization_barrier((low_rows, shares))
    load = jnp.concatenate([low_rows, first[piece:]], axis=0)
    came = [turn(load, "z", by) for by in steps]
    low_rows = ring_sum(load[:piece], [member[:piece] for member in came]).astype(bf16)
    extras = stacked([member[piece:] for member in [load] + came])
    extras_swapped = swap(extras)
    low_all = stacked([low_rows] + [turn(low_rows, "dp", by) for by in steps])
    down_grad, up_grad, bias_grad, beta_grad = run_small(
        at, low_all, swap(low_all), extras, extras_swapped
    )
    down_grad = down_grad.reshape(width, 128)
    bias_grad = bias_grad.reshape(1024)
    beta_grad = beta_grad.reshape(8, 8, 384)[:, :, :piece].reshape(8, width).T

    results = ring_sum(shares[0], [turn(shares[by], "head", by) for by in steps]).astype(bf16)
    layer_out = results[0].T[None]
    input_grad = results[1].T[None]

    moved = lax.all_to_all(
        summed.reshape(8, piece // 4, 512), ("z", "core"), 0, 0, tiled=True
    )
    qkv_grad, out_grad = run_place(moved)
    qkv_grad = jnp.swapaxes(qkv_grad, 0, 1)
    return (layer_out, input_grad, qkv_grad, out_grad, up_grad, down_grad, beta_grad, bias_grad)


def solution(mesh):
    fine = Mesh(
        mesh.devices.reshape(4, 2, mesh.shape["dp"], mesh.shape["head"]),
        ("z", "core", "dp", "head"),
    )
    context = ("z", "core")
    return jax.shard_map(
        shards,
        mesh=fine,
        in_specs=(
            P("dp", context, "head"),
            P("dp", context, "head"),
            P(None, None, "head"),
            P(None, "head"),
            P(),
            P(None, "head"),
            P(None, "head"),
            P("head"),
        ),
        out_specs=(
            P("dp", context, "head"),
            P("dp", context, "head"),
            P(context + ("dp",), None, "head"),
            P(context + ("dp",), "head"),
            P(None, "head"),
            P(),
            P(None, "head"),
            P("head"),
        ),
        check_vma=False,
    )
```
